512 devices in a mesh: lon: 32 (over y_hi, z, core), lat: 16 (over y_lo, x).
Axes of the slice: x: 4, y: 8 (y_hi: 2, y_lo: 4; y = y_hi * 4 + y_lo), z: 8, core: 2. Of those that a mesh axis runs over, the one named last changes fastest.
Arguments:
- tracer_adjoint: bfloat16 [512, 64, 64, 128], P('lat', 'lon'), may hold values from -6 to 6
- tracer_old: bfloat16 [512, 64, 64, 128], P('lat', 'lon'), may hold values from -6 to 6
- owner_lon: int32 [512, 64], P('lat', 'lon'), may hold values from 0 to 31, as said below
- row_step: int32 [512, 64], P('lat', 'lon'), may hold values from 0 to 2
- owner_column: int32 [512, 64], P('lat', 'lon'), may hold values from 0 to 1
- tile_kind: int32 [512, 64], P('lat', 'lon'), may hold values from 0 to 3
- blend_weights: bfloat16 [4, 128, 128], replicated, may hold values from -0.5 to 0.5
- slope_east: bfloat16 [4, 128, 128], replicated, may hold values from -0.0625 to 0.0625
- slope_north: bfloat16 [4, 128, 128], replicated, may hold values from -0.0625 to 0.0625
Outputs:
- tracer_old_adjoint: bfloat16 [512, 64, 64, 128], P('lat', 'lon')
- wind_sensitivity: float32 [512, 64, 2, 128], P('lat', 'lon')
The draws below stay inside these ranges and needn't reach their ends.
Inputs may be any that keep to these rules, and one draw needn't show every extreme that they name: `owner_lon`: A tile of longitude device h names h itself or a device h + d modulo 32 with 1 <= d <= 16 or 1 <= -d < 16, the reach growing from the equatorial row groups to the polar ones. Among the tiles of one device (rows 32 g to 32 g + 31, tile columns 2 h to 2 h + 1) at most 4 name any one longitude device other than h; for every group of 32 rows one other longitude device is named exactly 4 times by the tiles of every device of that group, in the two polar groups the device h + 16.
All inputs are finite; a program needn't handle non-finite values.
Results may differ from the reference program's by a relative error of at most 0.0075.
Values may be sent and summed in bfloat16 or wider, within the bound.
No kernel may reach another device: no remote copies, remote signals or barrier semaphores. Data moves between devices by JAX's collectives and lax.ppermute only.
A program may use at most 128 MiB of HBM per device.

```python
import jax
import jax.numpy as jnp
from jax import lax

BLOCK = 128
BC = 2
BR = 32
LEV = 64
NCLASS = 4
CAP = 4
NROWS = 512
NCOLS = 64
N_LON = 32
N_LAT = 16


def draw_owner_lon(key, part):
    tiles_here = BR * BC
    far_most = N_LON // 2
    listed = (2 * far_most - 1) * CAP
    key_hot, key_side, key_rest = jax.random.split(key, 3)
    groups = jnp.arange(N_LAT, dtype=jnp.int32)
    reach = jnp.maximum(1, far_most * jnp.abs(2 * groups + 1 - N_LAT) // max(N_LAT - 1, 1)).astype(jnp.int32)
    hot_dist = 1 + jax.random.randint(key_hot, (N_LAT,), 0, 1 << 20) % reach
    hot_dist = jnp.where(reach >= far_most, far_most, hot_dist)
    hot_sign = jax.random.randint(key_side, (N_LAT,), 0, 2) * 2 - 1
    hot_sign = jnp.where(hot_dist >= far_most, 1, hot_sign)
    hot_offset = (hot_sign * hot_dist).astype(jnp.int32)
    device_keys = jax.random.split(key_rest, N_LAT * N_LON)
    slot_ids = jnp.arange(listed, dtype=jnp.int32)
    slot_group = slot_ids // CAP
    slot_offset = jnp.where(slot_group < far_most - 1, slot_group - far_most + 1, slot_group - far_most + 2).astype(jnp.int32)
    positions = jnp.arange(tiles_here, dtype=jnp.int32)

    def one_device(device_key, group_reach, favoured, column_dev):
        first_key, second_key = jax.random.split(device_key)
        valid = (jnp.abs(slot_offset) <= group_reach) & (slot_offset != favoured)
        order_key = jnp.where(valid, 0, listed) + jax.random.permutation(first_key, listed).astype(jnp.int32)
        ordered = slot_offset[jnp.argsort(order_key, stable=True)]
        remote_count = jnp.minimum(tiles_here, 2 * group_reach * CAP - CAP)
        picked = ordered[jnp.clip(positions - CAP, 0, listed - 1)]
        offsets = jnp.where(positions < CAP, favoured, jnp.where(positions < remote_count, picked, 0))
        offsets = jax.random.permutation(second_key, offsets.astype(jnp.int32))
        return ((column_dev + offsets) % N_LON).astype(jnp.int32)
    reach_all = jnp.repeat(reach, N_LON)
    favoured_all = jnp.repeat(hot_offset, N_LON)
    column_all = jnp.tile(jnp.arange(N_LON, dtype=jnp.int32), N_LAT)
    blocks = jax.vmap(one_device)(device_keys, reach_all, favoured_all, column_all)
    blocks = blocks.reshape(N_LAT, N_LON, BR, BC).transpose(0, 2, 1, 3)
    return blocks.reshape(NROWS, NCOLS).astype(jnp.int32)


def place_ends(array, rng, smallest, high):
    shape = array.shape
    spot = [jax.random.randint(jax.random.fold_in(rng, axis), (), 0, shape[axis]) for axis in range(len(shape))]
    array = array.at[tuple(spot)].set(smallest)
    longest = shape.index(max(shape))
    spot[longest] = (spot[longest] + 1) % shape[longest]
    return array.at[tuple(spot)].set(high)


def level_of(own_key, shape, cuts, smallest, top_value):
    level = 1.0
    for dim, parts in cuts:
        heights = jax.random.uniform(jax.random.fold_in(jax.random.fold_in(own_key, 6), dim), (parts,), jnp.float32, smallest / len(cuts), top_value / len(cuts))
        level = level * jnp.repeat(jnp.exp(heights), shape[dim] // parts).reshape((-1,) + (1,) * (len(shape) - 1 - dim))
    return level


def normal_values(key, dims, deviation, most, cuts=(), held_as=jnp.bfloat16):
    drawn = deviation * jax.random.normal(key, dims, jnp.float32)
    if cuts:
        drawn = drawn * level_of(key, dims, cuts, -0.22, 0.18)
    return jnp.clip(drawn, -most, most).astype(held_as)


def setup_inputs(seed: int = 0) -> dict:
    key_of = jax.random.split(jax.random.key(seed), 10)
    tracer_adjoint = normal_values(key_of[0], (NROWS, NCOLS, LEV, BLOCK), 1.0, 6.0, ((0, 16), (1, 32)))
    tracer_old = normal_values(key_of[1], (NROWS, NCOLS, LEV, BLOCK), 1.0, 6.0, ((0, 16), (1, 32)))
    owner_lon = draw_owner_lon(jax.random.fold_in(key_of[9], 71), 0)
    row_step = place_ends(jax.random.randint(key_of[3], (NROWS, NCOLS), 0, 3), jax.random.fold_in(key_of[3], 1), 0, 2).astype(jnp.int32)
    owner_column = place_ends(jax.random.randint(key_of[4], (NROWS, NCOLS), 0, BC), jax.random.fold_in(key_of[4], 1), 0, BC - 1).astype(jnp.int32)
    tile_kind = place_ends(jax.random.randint(key_of[5], (NROWS, NCOLS), 0, NCLASS), jax.random.fold_in(key_of[5], 1), 0, NCLASS - 1).astype(jnp.int32)
    blend_weights = normal_values(key_of[6], (NCLASS, BLOCK, BLOCK), BLOCK ** -0.5, 0.5)
    slope_east = normal_values(key_of[7], (NCLASS, BLOCK, BLOCK), (BLOCK * LEV) ** -0.5, 0.0625)
    slope_north = normal_values(key_of[8], (NCLASS, BLOCK, BLOCK), (BLOCK * LEV) ** -0.5, 0.0625)
    return dict(tracer_adjoint=tracer_adjoint, tracer_old=tracer_old, owner_lon=owner_lon, row_step=row_step, owner_column=owner_column, tile_kind=tile_kind, blend_weights=blend_weights, slope_east=slope_east, slope_north=slope_north)


def reference(tracer_adjoint, tracer_old, owner_lon, row_step, owner_column, tile_kind, blend_weights, slope_east, slope_north):
    zero_row = jnp.zeros((1, NCOLS, LEV, BLOCK), tracer_old.dtype)
    padded = jnp.concatenate([zero_row, tracer_old, zero_row], axis=0)
    blend_full = blend_weights.astype(jnp.float32)
    east_full = slope_east.astype(jnp.float32)
    north_full = slope_north.astype(jnp.float32)
    row_ids = jnp.arange(NROWS, dtype=jnp.int32)

    def tile_row(row_index):
        source_row = (row_index + row_step[row_index]).astype(jnp.int32)
        column = (owner_lon[row_index] * BC + owner_column[row_index]).astype(jnp.int32)
        source = padded[source_row, column].astype(jnp.float32)
        kinds = tile_kind[row_index]
        adjoint_row = tracer_adjoint[row_index].astype(jnp.float32)
        east = jnp.einsum("tlm,tma->tla", source, east_full[kinds])
        north = jnp.einsum("tlm,tma->tla", source, north_full[kinds])
        sensed = jnp.stack([jnp.sum(adjoint_row * east, axis=1), jnp.sum(adjoint_row * north, axis=1)], axis=1)
        spread = jnp.einsum("tla,tma->tlm", adjoint_row, blend_full[kinds]).astype(jnp.bfloat16)
        return spread, sensed

    spread_all, sensitivity = lax.map(tile_row, row_ids)

    def target_row(target):
        own_sum = jnp.zeros((NCOLS, LEV, BLOCK), jnp.float32)
        cross_sum = jnp.zeros((NCOLS, LEV, BLOCK), jnp.float32)
        for offset in (-1, 0, 1):
            anchor = target - offset
            inside = (anchor >= 0) & (anchor < NROWS)
            anchor_c = jnp.clip(anchor, 0, NROWS - 1).astype(jnp.int32)
            chosen = (row_step[anchor_c] == offset + 1) & inside
            column = (owner_lon[anchor_c] * BC + owner_column[anchor_c]).astype(jnp.int32)
            values = jnp.where(chosen[:, None, None], spread_all[anchor_c].astype(jnp.float32), 0.0)
            part_sum = jax.ops.segment_sum(values, column, num_segments=NCOLS)
            crossing = (target // BR) != (anchor_c // BR)
            own_sum = own_sum + jnp.where(crossing, 0.0, part_sum)
            cross_sum = cross_sum + jnp.where(crossing, part_sum, 0.0)
        rounded = lax.optimization_barrier(cross_sum.astype(jnp.bfloat16))
        return (own_sum + rounded.astype(jnp.float32)).astype(jnp.bfloat16)

    adjoint_old = lax.map(target_row, row_ids)
    return adjoint_old, sensitivity
```

```python
import functools

import jax
import jax.numpy as jnp
from jax import lax
from jax.experimental import pallas as pl
from jax.experimental.pallas import tpu as pltpu
from jax.sharding import PartitionSpec as P

CAP = 4
UNROLL = 4
KINDS = 4


def pack_kernel(owner, step, column, kind, adjoint, send, places, codes, counts, tiles, load_sem, sem):
    tile_cols, tile_rows = owner.shape
    tiles_here, levels, _ = adjoint.shape
    lon_count = counts.shape[0]
    me = lax.axis_index("lon")
    load = pltpu.make_async_copy(adjoint, tiles, load_sem)
    load.start()

    for d in range(lon_count):
        counts[d] = 0
        for r in range(CAP):
            codes[d * CAP + r] = 0

    def place_row(i, sent):
        for j in range(tile_cols):
            to = owner[j, i]
            rank = counts[to]
            counts[to] = rank + 1
            block = (i + step[j, i]) * tile_cols + column[j, i]
            code = block * KINDS + kind[j, i] + 1
            remote = to != me
            slot = jnp.where(remote, to * CAP + rank, lon_count * CAP)
            codes[slot] = code
            places[i * tile_cols + j] = jnp.where(remote, slot, -code)
            sent = sent + remote.astype(jnp.int32)
        return sent

    sent = lax.fori_loop(0, tile_rows, place_row, 0)
    load.wait()

    def send_row(i, carry):
        for j in range(tile_cols):
            tile = i * tile_cols + j
            slot = places[tile]

            @pl.when(slot >= 0)
            def _():
                pltpu.make_async_copy(tiles.at[tile], send.at[slot], sem).start()

        return carry

    lax.fori_loop(0, tile_rows, send_row, 0)

    def settle(_, carry):
        pltpu.make_async_copy(tiles.at[0], send.at[0], sem).wait()
        return carry

    lax.fori_loop(0, sent, settle, 0)


def pack(owner, step, column, kind, adjoint, lon_count):
    tiles_here, levels, width = adjoint.shape
    smem = pl.BlockSpec(memory_space=pltpu.SMEM)
    hbm = pl.BlockSpec(memory_space=pltpu.HBM)
    return pl.pallas_call(
        pack_kernel,
        out_shape=(
            jax.ShapeDtypeStruct((lon_count * CAP, levels, width), jnp.bfloat16),
            jax.ShapeDtypeStruct((tiles_here,), jnp.int32),
            jax.ShapeDtypeStruct((lon_count * CAP + 128,), jnp.int32),
        ),
        in_specs=[smem, smem, smem, smem, hbm],
        out_specs=(hbm, smem, smem),
        scratch_shapes=[
            pltpu.SMEM((lon_count,), jnp.int32),
            pltpu.VMEM((tiles_here, levels, width), jnp.bfloat16),
            pltpu.SemaphoreType.DMA,
            pltpu.SemaphoreType.DMA,
        ],
        name="pack",
    )(owner, step, column, kind, adjoint)


def adjoint_kernel(
    places, codes, received, adjoint, old, before, after, blend, east, north,
    result, edge_own, cross_before, cross_after, sensed_remote, sensed_home,
    tiles, sources, sums, sensed, back, slopes, work, sem, out_sem,
):
    tiles_here, levels, width = adjoint.shape
    slot_count = received.shape[0]
    tile_cols = before.shape[0]
    block_count = tiles_here + 2 * tile_cols

    loads = [
        pltpu.make_async_copy(received, tiles.at[pl.ds(0, slot_count)], sem.at[0]),
        pltpu.make_async_copy(adjoint, tiles.at[pl.ds(slot_count, tiles_here)], sem.at[1]),
        pltpu.make_async_copy(old, sources.at[pl.ds(tile_cols, tiles_here)], sem.at[2]),
        pltpu.make_async_copy(before, sources.at[pl.ds(0, tile_cols)], sem.at[3]),
        pltpu.make_async_copy(after, sources.at[pl.ds(tile_cols + tiles_here, tile_cols)], sem.at[4]),
    ]
    for copy in loads:
        copy.start()

    def enlist(n, count):
        for u in range(8):
            s = n * 8 + u
            code = codes[s]
            work[count] = s * 512 + code - 1
            count = count + (code > 0).astype(jnp.int32)
        return count

    count = lax.fori_loop(0, slot_count // 8, enlist, 0)

    def enlist_home(n, count):
        for u in range(8):
            t = n * 8 + u
            place = places[t]
            work[count] = (slot_count + t) * 512 - place - 1
            count = count + (place < 0).astype(jnp.int32)
        return count

    count = lax.fori_loop(0, tiles_here // 8, enlist_home, count)
    for u in range(UNROLL):
        work[count + u] = (slot_count + tiles_here) * 512 + block_count * KINDS

    for k in range(KINDS):
        back[k] = blend[k].T
        slopes[k, :, :width] = east[k]
        slopes[k, :, width:] = north[k]
    sources[block_count] = jnp.zeros((levels, width), jnp.bfloat16)
    tiles[slot_count + tiles_here] = jnp.zeros((levels, width), jnp.bfloat16)

    def clear(b, carry):
        sums[b] = jnp.zeros((levels, width), jnp.float32)
        return carry

    lax.fori_loop(0, block_count + 1, clear, 0, unroll=3)
    for copy in loads:
        copy.wait()

    def some_tiles(n, carry):
        entries = [work[n * UNROLL + u] for u in range(UNROLL)]
        place = [e >> 9 for e in entries]
        kind = [e & (KINDS - 1) for e in entries]
        block = [(e & 511) >> 2 for e in entries]
        arrived = [tiles[p] for p in place]
        spread = [
            jnp.dot(a, back[k], preferred_element_type=jnp.float32) for a, k in zip(arrived, kind)
        ]
        slope = [
            jnp.dot(sources[b], slopes[k], preferred_element_type=jnp.float32) for b, k in zip(block, kind)
        ]
        for p, a, s in zip(place, arrived, slope):
            full = a.astype(jnp.float32)
            sensed[p, 0:1] = jnp.sum(full * s[:, :width], axis=0, keepdims=True)
            sensed[p, 1:2] = jnp.sum(full * s[:, width:], axis=0, keepdims=True)
        for b, s in zip(block, spread):
            sums[b] += s.astype(jnp.bfloat16).astype(jnp.float32)
        return carry

    lax.fori_loop(0, (count + UNROLL - 1) // UNROLL, some_tiles, 0)

    outs = [
        pltpu.make_async_copy(sensed.at[pl.ds(0, slot_count)], sensed_remote, out_sem.at[0]),
        pltpu.make_async_copy(sensed.at[pl.ds(slot_count, tiles_here)], sensed_home, out_sem.at[1]),
    ]
    for copy in outs:
        copy.start()
    for c in range(tile_cols):
        cross_before[c] = sums[c].astype(jnp.bfloat16)
        cross_after[c] = sums[tile_cols + tiles_here + c].astype(jnp.bfloat16)
        edge_own[c] = sums[tile_cols + c]
        edge_own[tile_cols + c] = sums[tiles_here + c]

    def finish(b, carry):
        result[b] = sums[tile_cols + b].astype(jnp.bfloat16)
        return carry

    lax.fori_loop(0, tiles_here, finish, 0, unroll=4)
    for copy in outs:
        copy.wait()


def adjoint_step(places, codes, received, adjoint, old, before, after, blend, east, north):
    slot_count = received.shape[0]
    tiles_here, levels, width = adjoint.shape
    tile_cols = before.shape[0]
    block_count = tiles_here + 2 * tile_cols
    smem = pl.BlockSpec(memory_space=pltpu.SMEM)
    vmem = pl.BlockSpec(memory_space=pltpu.VMEM)
    hbm = pl.BlockSpec(memory_space=pltpu.HBM)
    edge = jax.ShapeDtypeStruct((tile_cols, levels, width), jnp.bfloat16)
    return pl.pallas_call(
        adjoint_kernel,
        out_shape=(
            jax.ShapeDtypeStruct((tiles_here, levels, width), jnp.bfloat16),
            jax.ShapeDtypeStruct((2 * tile_cols, levels, width), jnp.float32),
            edge,
            edge,
            jax.ShapeDtypeStruct((slot_count, 2, width), jnp.float32),
            jax.ShapeDtypeStruct((tiles_here, 2, width), jnp.float32),
        ),
        in_specs=[smem, smem, hbm, hbm, hbm, hbm, hbm, vmem, vmem, vmem],
        out_specs=(vmem, vmem, vmem, vmem, hbm, hbm),
        scratch_shapes=[
            pltpu.VMEM((slot_count + tiles_here + 1, levels, width), jnp.bfloat16),
            pltpu.VMEM((block_count + 1, levels, width), jnp.bfloat16),
            pltpu.VMEM((block_count + 1, levels, width), jnp.float32),
            pltpu.VMEM((slot_count + tiles_here + 1, 2, width), jnp.float32),
            pltpu.VMEM((KINDS, width, width), jnp.bfloat16),
            pltpu.VMEM((KINDS, width, 2 * width), jnp.bfloat16),
            pltpu.SMEM((slot_count + tiles_here + UNROLL,), jnp.int32),
            pltpu.SemaphoreType.DMA((5,)),
            pltpu.SemaphoreType.DMA((2,)),
        ],
        compiler_params=pltpu.CompilerParams(vmem_limit_bytes=32 * 1024 * 1024),
        name="adjoint",
    )(places, codes, received, adjoint, old, before, after, blend, east, north)


def finish_kernel(places, returned, sensed_home, edge_own, from_before, from_after, _, result, sensed, edges, sem):
    tiles_here = sensed.shape[0]
    tile_cols = from_before.shape[0]
    for c in range(tile_cols):
        edges[c] = (edge_own[c] + from_before[c].astype(jnp.float32)).astype(jnp.bfloat16)
        edges[tile_cols + c] = (edge_own[tile_cols + c] + from_after[c].astype(jnp.float32)).astype(jnp.bfloat16)
    copies = [
        pltpu.make_async_copy(edges.at[pl.ds(0, tile_cols)], result.at[pl.ds(0, tile_cols)], sem.at[0]),
        pltpu.make_async_copy(
            edges.at[pl.ds(tile_cols, tile_cols)], result.at[pl.ds(tiles_here - tile_cols, tile_cols)], sem.at[1]
        ),
    ]
    for copy in copies:
        copy.start()

    def place_one(t, carry):
        place = places[t]
        sensed[t] = jnp.where(place < 0, sensed_home[t], returned[jnp.maximum(place, 0)])
        return carry

    lax.fori_loop(0, tiles_here, place_one, 0)
    for copy in copies:
        copy.wait()


def finish(places, returned, sensed_home, edge_own, from_before, from_after, partial):
    tiles_here, _, width = sensed_home.shape
    smem = pl.BlockSpec(memory_space=pltpu.SMEM)
    vmem = pl.BlockSpec(memory_space=pltpu.VMEM)
    hbm = pl.BlockSpec(memory_space=pl.ANY)
    return pl.pallas_call(
        finish_kernel,
        out_shape=(
            jax.ShapeDtypeStruct(partial.shape, partial.dtype),
            jax.ShapeDtypeStruct((tiles_here, 2, width), jnp.float32),
        ),
        in_specs=[smem, vmem, vmem, vmem, vmem, vmem, hbm],
        out_specs=(hbm, vmem),
        scratch_shapes=[
            pltpu.VMEM(edge_own.shape, jnp.bfloat16),
            pltpu.SemaphoreType.DMA((2,)),
        ],
        input_output_aliases={6: 0},
        name="finish",
    )(places, returned, sensed_home, edge_own, from_before, from_after, partial)


def on_device(
    tracer_adjoint, tracer_old, owner_lon, row_step, owner_column, tile_kind, blend_weights, slope_east, slope_north
):
    lon_count = lax.axis_size("lon")
    lat_count = lax.axis_size("lat")
    tile_rows, tile_cols = owner_lon.shape
    levels, width = tracer_adjoint.shape[2:]
    tiles_here = tile_rows * tile_cols
    north_to_south = [(i, i + 1) for i in range(lat_count - 1)]
    south_to_north = [(j, i) for i, j in north_to_south]
    adjoint = tracer_adjoint.reshape(tiles_here, levels, width)
    old = tracer_old.reshape(tiles_here, levels, width)

    send, places, codes = pack(owner_lon.T, row_step.T, owner_column.T, tile_kind.T, adjoint, lon_count)
    received = lax.all_to_all(send, "lon", split_axis=0, concat_axis=0, tiled=True)
    before = lax.ppermute(old[-tile_cols:], "lat", north_to_south)
    after = lax.ppermute(old[:tile_cols], "lat", south_to_north)
    asked = lax.all_to_all(codes[: lon_count * CAP], "lon", split_axis=0, concat_axis=0, tiled=True)
    partial, edge_own, cross_before, cross_after, sensed_remote, sensed_home = adjoint_step(
        places, asked, received, adjoint, old, before, after, blend_weights, slope_east, slope_north
    )
    returned = lax.all_to_all(sensed_remote, "lon", split_axis=0, concat_axis=0, tiled=True)
    from_after = lax.ppermute(cross_before, "lat", south_to_north)
    from_before = lax.ppermute(cross_after, "lat", north_to_south)
    result, sensed = finish(places, returned, sensed_home, edge_own, from_before, from_after, partial)
    return (
        result.reshape(tracer_old.shape),
        sensed.reshape(tile_rows, tile_cols, 2, width),
    )


def solution(mesh):
    return jax.shard_map(
        on_device,
        mesh=mesh,
        in_specs=(
            P("lat", "lon", None, None),
            P("lat", "lon", None, None),
            P("lat", "lon"),
            P("lat", "lon"),
            P("lat", "lon"),
            P("lat", "lon"),
            P(),
            P(),
            P(),
        ),
        out_specs=(P("lat", "lon", None, None), P("lat", "lon", None, None)),
        check_vma=False,
    )
```

```python
import functools

import jax
import jax.numpy as jnp
from jax import lax
from jax.experimental import pallas as pl
from jax.experimental.pallas import tpu as pltpu
from jax.sharding import PartitionSpec as P

CAP = 4
META = 16
KINDS = 4
CODES = 512
EXACT = 200
UNROLL = 8
PARTS = 4
VMEM_LIMIT = 24 * 1024 * 1024


def in_hbm(array):
    return pltpu.with_memory_space_constraint(array, pltpu.HBM)


def in_vmem(array):
    return pltpu.with_memory_space_constraint(array, pltpu.VMEM)


def pack_kernel(owner, step, column, kind, adjoint, send, places, codes, counts, tiles, meta, load_sem, sem, meta_sem):
    tile_cols, tile_rows = owner.shape
    tiles_here, levels, _ = adjoint.shape
    lon_count = counts.shape[0]
    me = lax.axis_index("lon")
    load = pltpu.make_async_copy(adjoint, tiles, load_sem)
    load.start()

    for d in range(lon_count):
        counts[d] = 0
        for r in range(CAP):
            codes[d * CAP + r] = 0

    def place_rows(n, sent):
        for u in range(4):
            i = n * 4 + u
            for j in range(tile_cols):
                to = owner[j, i]
                rank = counts[to]
                remote = to != me
                counts[to] = rank + 1
                block = (i + step[j, i]) * tile_cols + column[j, i]
                code = block * KINDS + kind[j, i] + 1
                places[i * tile_cols + j] = jnp.where(remote, to * CAP + rank, -code)
                codes[jnp.where(remote, to * CAP + rank, me * CAP)] = jnp.where(remote, code, 0)
                sent = sent + remote.astype(jnp.int32)
        return sent

    sent = lax.fori_loop(0, tile_rows // 4, place_rows, 0)
    load.wait()

    def send_rows(n, carry):
        for u in range(8):
            tile = n * 8 + u
            slot = places[tile]

            @pl.when(slot >= 0)
            def _():
                rows = pl.ds(pl.multiple_of((slot & (CAP - 1)) * levels, levels), levels)
                pltpu.make_async_copy(tiles.at[tile], send.at[slot // CAP, rows, :], sem).start()

        return carry

    lax.fori_loop(0, tiles_here // 8, send_rows, 0)
    lane = lax.broadcasted_iota(jnp.int32, (META, 128), 1)

    def describe(n, carry):
        for u in range(4):
            d = n * 4 + u
            line = jnp.zeros((META, 128), jnp.int32)
            for r in range(CAP):
                code = codes[d * CAP + r]
                line = jnp.where(lane == r, jnp.where(code > EXACT, EXACT - code, code), line)
            meta[d] = line.astype(jnp.float32).astype(jnp.bfloat16)
        return carry

    lax.fori_loop(0, lon_count // 4, describe, 0)
    told = pltpu.make_async_copy(meta, send.at[:, pl.ds(CAP * levels, META), :], meta_sem)
    told.start()

    def settle(_, carry):
        pltpu.make_async_copy(tiles.at[0], send.at[0, pl.ds(0, levels), :], sem).wait()
        return carry

    lax.fori_loop(0, sent, settle, 0)
    told.wait()


def pack(owner, step, column, kind, adjoint, lon_count):
    tiles_here, levels, width = adjoint.shape
    smem = pl.BlockSpec(memory_space=pltpu.SMEM)
    hbm = pl.BlockSpec(memory_space=pltpu.HBM)
    return pl.pallas_call(
        pack_kernel,
        out_shape=(
            pltpu.HBM((lon_count, CAP * levels + META, width), jnp.bfloat16),
            jax.ShapeDtypeStruct((tiles_here,), jnp.int32),
        ),
        in_specs=[smem, smem, smem, smem, hbm],
        out_specs=(hbm, smem),
        scratch_shapes=[
            pltpu.SMEM((lon_count * CAP,), jnp.int32),
            pltpu.SMEM((lon_count,), jnp.int32),
            pltpu.VMEM((tiles_here, levels, width), jnp.bfloat16),
            pltpu.VMEM((lon_count, META, width), jnp.bfloat16),
            pltpu.SemaphoreType.DMA,
            pltpu.SemaphoreType.DMA,
            pltpu.SemaphoreType.DMA,
        ],
        compiler_params=pltpu.CompilerParams(vmem_limit_bytes=60 * 1024 * 1024),
        name="pack",
    )(owner, step, column, kind, in_hbm(adjoint))


def adjoint_kernel(
    places, received, adjoint, old, before, after, blend, east, north,
    result, edge_own, cross_before, cross_after, sensed_remote, sensed_home,
    tiles, sources, sums, remote, home, rounded, edges, back, slopes, listed, codes, work, counts,
    sem, code_sem, out_sem,
):
    lon_count = received.shape[0]
    tiles_here, levels, width = adjoint.shape
    slot_count = lon_count * CAP
    tile_cols = before.shape[0]
    block_count = tiles_here + 2 * tile_cols
    room = work.shape[0] // (2 * KINDS)
    me = lax.axis_index("lon")

    line = received[:, CAP * levels : CAP * levels + META, :].astype(jnp.float32)[:, 0, :].astype(jnp.int32)
    listed[...] = jnp.where(line < 0, EXACT - line, line)
    code_copy = pltpu.make_async_copy(listed, codes, code_sem)
    code_copy.start()
    loads = [
        pltpu.make_async_copy(old, sources.at[pl.ds(tile_cols, tiles_here)], sem.at[0]),
        pltpu.make_async_copy(before, sources.at[pl.ds(0, tile_cols)], sem.at[1]),
        pltpu.make_async_copy(after, sources.at[pl.ds(tile_cols + tiles_here, tile_cols)], sem.at[2]),
        pltpu.make_async_copy(adjoint, tiles, sem.at[3]),
    ]
    for copy in loads:
        copy.start()
    for k in range(KINDS):
        back[k] = blend[k].T
        slopes[k, :, :width] = east[k]
        slopes[k, :, width:] = north[k]

    def clear(b, carry):
        sums[b] = jnp.zeros((levels, width), jnp.float32)
        return carry

    lax.fori_loop(0, block_count + 1, clear, 0, unroll=3)

    for k in range(2 * KINDS):
        counts[k] = 0

    def enlist(where, entry, code, valid):
        row = where * KINDS + (code & (KINDS - 1))
        n = counts[row]
        work[row * room + n] = entry * CODES + code
        counts[row] = n + valid.astype(jnp.int32)

    def enlist_home(n, carry):
        for u in range(8):
            place = places[n * 8 + u]
            enlist(1, n * 8 + u, -place - 1, place < 0)
        return carry

    lax.fori_loop(0, tiles_here // 8, enlist_home, 0)
    code_copy.wait()

    def enlist_remote(n, carry):
        for u in range(2):
            s = n * 2 + u
            for r in range(CAP):
                code = codes[s, r]
                enlist(0, s * CAP + r, code - 1, (code > 0) & (s != me))
        return carry

    lax.fori_loop(0, lon_count // 2, enlist_remote, 0)
    for k in range(KINDS):
        for where, spare in ((0, slot_count), (1, tiles_here)):
            row = where * KINDS + k
            n = counts[row]
            for u in range(UNROLL):
                work[row * room + n + u] = spare * CODES + block_count * KINDS + k
    for copy in loads:
        copy.wait()

    def arrived_tile(p):
        p = jnp.minimum(p, slot_count - 1)
        rows = pl.ds(pl.multiple_of((p & (CAP - 1)) * levels, levels), levels)
        return received[p // CAP, rows, :]

    def home_tile(p):
        return tiles[jnp.minimum(p, tiles_here - 1)]

    def some_tiles(row, kind, tile_at, sensed, n):
        entries = [work[row * room + n * UNROLL + u] for u in range(UNROLL)]
        place = [e // CODES for e in entries]
        block = [(e & (CODES - 1)) // KINDS for e in entries]
        arrived = [tile_at(p) for p in place]
        source = [sources[jnp.minimum(b, block_count - 1)] for b in block]
        spread = jnp.dot(jnp.concatenate(arrived, axis=0), back[kind], preferred_element_type=jnp.float32)
        slope = jnp.dot(jnp.concatenate(source, axis=0), slopes[kind], preferred_element_type=jnp.float32)
        for u in range(UNROLL):
            full = arrived[u].astype(jnp.float32)
            s = slope[u * levels : (u + 1) * levels]
            sensed[place[u], 0:1] = jnp.sum(full * s[:, :width], axis=0, keepdims=True)
            sensed[place[u], 1:2] = jnp.sum(full * s[:, width:], axis=0, keepdims=True)
        for u in range(UNROLL):
            s = spread[u * levels : (u + 1) * levels]
            sums[block[u]] += s.astype(jnp.bfloat16).astype(jnp.float32)

    for where, tile_at, sensed in ((0, arrived_tile, remote), (1, home_tile, home)):
        for kind in range(KINDS):
            row = where * KINDS + kind

            def step(n, carry, row=row, kind=kind, tile_at=tile_at, sensed=sensed):
                some_tiles(row, kind, tile_at, sensed, n)
                return carry

            lax.fori_loop(0, (counts[row] + UNROLL - 1) // UNROLL, step, 0)

    copies = []

    def put(source, target):
        copy = pltpu.make_async_copy(source, target, out_sem.at[len(copies)])
        copy.start()
        copies.append(copy)

    put(remote.at[pl.ds(0, slot_count)], sensed_remote)
    put(home.at[pl.ds(0, tiles_here)], sensed_home)
    for c in range(tile_cols):
        edges[c] = sums[c].astype(jnp.bfloat16)
        edges[tile_cols + c] = sums[tile_cols + tiles_here + c].astype(jnp.bfloat16)
    put(edges.at[pl.ds(0, tile_cols)], cross_before)
    put(edges.at[pl.ds(tile_cols, tile_cols)], cross_after)
    put(sums.at[pl.ds(tile_cols, tile_cols)], edge_own.at[pl.ds(0, tile_cols)])
    put(sums.at[pl.ds(tiles_here, tile_cols)], edge_own.at[pl.ds(tile_cols, tile_cols)])

    def finish(b, carry):
        rounded[b] = sums[tile_cols + b].astype(jnp.bfloat16)
        return carry

    part = tiles_here // PARTS
    for p in range(PARTS):
        lax.fori_loop(p * part, (p + 1) * part, finish, 0, unroll=4)
        put(rounded.at[pl.ds(p * part, part)], result.at[pl.ds(p * part, part)])
    for copy in copies:
        copy.wait()


def adjoint_step(places, received, adjoint, old, before, after, blend, east, north):
    lon_count = received.shape[0]
    slot_count = lon_count * CAP
    tiles_here, levels, width = adjoint.shape
    tile_cols = before.shape[0]
    block_count = tiles_here + 2 * tile_cols
    assert (block_count + 1) * KINDS <= CODES and block_count * KINDS <= EXACT + 256
    smem = pl.BlockSpec(memory_space=pltpu.SMEM)
    vmem = pl.BlockSpec(memory_space=pltpu.VMEM)
    hbm = pl.BlockSpec(memory_space=pltpu.HBM)
    edge = pltpu.HBM((tile_cols, levels, width), jnp.bfloat16)
    return pl.pallas_call(
        adjoint_kernel,
        out_shape=(
            pltpu.HBM((tiles_here, levels, width), jnp.bfloat16),
            pltpu.HBM((2 * tile_cols, levels, width), jnp.float32),
            edge,
            edge,
            pltpu.HBM((slot_count, 2, width), jnp.float32),
            pltpu.HBM((tiles_here, 2, width), jnp.float32),
        ),
        in_specs=[smem, vmem, hbm, hbm, hbm, hbm, vmem, vmem, vmem],
        out_specs=(hbm,) * 6,
        scratch_shapes=[
            pltpu.VMEM((tiles_here, levels, width), jnp.bfloat16),
            pltpu.VMEM((block_count, levels, width), jnp.bfloat16),
            pltpu.VMEM((block_count + 1, levels, width), jnp.float32),
            pltpu.VMEM((slot_count + 1, 2, width), jnp.float32),
            pltpu.VMEM((tiles_here + 1, 2, width), jnp.float32),
            pltpu.VMEM((tiles_here, levels, width), jnp.bfloat16),
            pltpu.VMEM((2 * tile_cols, levels, width), jnp.bfloat16),
            pltpu.VMEM((KINDS, width, width), jnp.bfloat16),
            pltpu.VMEM((KINDS, width, 2 * width), jnp.bfloat16),
            pltpu.VMEM((lon_count, width), jnp.int32),
            pltpu.SMEM((lon_count, width), jnp.int32),
            pltpu.SMEM((2 * KINDS * (slot_count + UNROLL),), jnp.int32),
            pltpu.SMEM((2 * KINDS,), jnp.int32),
            pltpu.SemaphoreType.DMA((4,)),
            pltpu.SemaphoreType.DMA,
            pltpu.SemaphoreType.DMA((6 + PARTS,)),
        ],
        compiler_params=pltpu.CompilerParams(vmem_limit_bytes=VMEM_LIMIT),
        name="adjoint",
    )(places, in_vmem(received), in_hbm(adjoint), in_hbm(old), in_hbm(before), in_hbm(after), blend, east, north)


def finish_kernel(places, returned, sensed_home, edge_own, from_before, from_after, _, result, sensed, edges, out, sem):
    tiles_here = sensed.shape[0]
    tile_cols = from_before.shape[0]
    for c in range(tile_cols):
        edges[c] = (edge_own[c] + from_before[c].astype(jnp.float32)).astype(jnp.bfloat16)
        edges[tile_cols + c] = (edge_own[tile_cols + c] + from_after[c].astype(jnp.float32)).astype(jnp.bfloat16)
    copies = [
        pltpu.make_async_copy(edges.at[pl.ds(0, tile_cols)], result.at[pl.ds(0, tile_cols)], sem.at[0]),
        pltpu.make_async_copy(
            edges.at[pl.ds(tile_cols, tile_cols)],
            result.at[pl.ds(tiles_here - tile_cols, tile_cols)],
            sem.at[1],
        ),
        pltpu.make_async_copy(out, sensed, sem.at[2]),
    ]
    copies[0].start()
    copies[1].start()

    def place_some(n, carry):
        for u in range(8):
            t = n * 8 + u
            place = places[t]
            out[t] = jnp.where(place < 0, sensed_home[t], returned[jnp.maximum(place, 0)])
        return carry

    lax.fori_loop(0, tiles_here // 8, place_some, 0)
    copies[2].start()
    for copy in copies:
        copy.wait()


def finish(places, returned, sensed_home, edge_own, from_before, from_after, partial):
    tiles_here, _, width = sensed_home.shape
    smem = pl.BlockSpec(memory_space=pltpu.SMEM)
    vmem = pl.BlockSpec(memory_space=pltpu.VMEM)
    hbm = pl.BlockSpec(memory_space=pltpu.HBM)
    return pl.pallas_call(
        finish_kernel,
        out_shape=(
            jax.ShapeDtypeStruct(partial.shape, partial.dtype),
            jax.ShapeDtypeStruct((tiles_here, 2, width), jnp.float32),
        ),
        in_specs=[smem] + [vmem] * 5 + [hbm],
        out_specs=(hbm, hbm),
        scratch_shapes=[
            pltpu.VMEM(edge_own.shape, jnp.bfloat16),
            pltpu.VMEM((tiles_here, 2, width), jnp.float32),
            pltpu.SemaphoreType.DMA((3,)),
        ],
        input_output_aliases={6: 0},
        compiler_params=pltpu.CompilerParams(vmem_limit_bytes=8 * 1024 * 1024),
        name="finish",
    )(places, returned, sensed_home, edge_own, from_before, from_after, partial)


def on_device(
    tracer_adjoint, tracer_old, owner_lon, row_step, owner_column, tile_kind, blend_weights, slope_east, slope_north
):
    lon_count = lax.axis_size("lon")
    lat_count = lax.axis_size("lat")
    tile_rows, tile_cols = owner_lon.shape
    levels, width = tracer_adjoint.shape[2:]
    tiles_here = tile_rows * tile_cols
    north_to_south = [(i, i + 1) for i in range(lat_count - 1)]
    south_to_north = [(j, i) for i, j in north_to_south]
    adjoint = tracer_adjoint.reshape(tiles_here, levels, width)
    old = tracer_old.reshape(tiles_here, levels, width)

    send, places = pack(owner_lon.T, row_step.T, owner_column.T, tile_kind.T, adjoint, lon_count)
    received = lax.all_to_all(send, "lon", split_axis=0, concat_axis=0, tiled=True)
    before = lax.ppermute(old[-tile_cols:], "lat", north_to_south)
    after = lax.ppermute(old[:tile_cols], "lat", south_to_north)
    partial, edge_own, cross_before, cross_after, sensed_remote, sensed_home = adjoint_step(
        places, received, adjoint, old, before, after, blend_weights, slope_east, slope_north
    )
    returned = lax.all_to_all(sensed_remote, "lon", split_axis=0, concat_axis=0, tiled=True)
    from_after = lax.ppermute(cross_before, "lat", south_to_north)
    from_before = lax.ppermute(cross_after, "lat", north_to_south)
    result, sensed = finish(places, returned, sensed_home, edge_own, from_before, from_after, partial)
    return (
        result.reshape(tracer_old.shape),
        sensed.reshape(tile_rows, tile_cols, 2, width),
    )


def solution(mesh):
    return jax.shard_map(
        on_device,
        mesh=mesh,
        in_specs=(
            P("lat", "lon", None, None),
            P("lat", "lon", None, None),
            P("lat", "lon"),
            P("lat", "lon"),
            P("lat", "lon"),
            P("lat", "lon"),
            P(),
            P(),
            P(),
        ),
        out_specs=(P("lat", "lon", None, None), P("lat", "lon", None, None)),
        check_vma=False,
    )
```

```python
import functools

import jax
import jax.numpy as jnp
from jax import lax
from jax.experimental import pallas as pl
from jax.experimental.pallas import tpu as pltpu
from jax.sharding import PartitionSpec as P

CAP = 4
META = 16
KINDS = 4
CODES = 512
EXACT = 200
UNROLL = 8
PARTS = 4
VMEM_LIMIT = 24 * 1024 * 1024


def in_hbm(array):
    return pltpu.with_memory_space_constraint(array, pltpu.HBM)


def in_vmem(array):
    return pltpu.with_memory_space_constraint(array, pltpu.VMEM)


def pack_kernel(
    owner_all, step_all, column_all, kind_all, adjoint, send, places,
    owner, step, column, kind, codes, counts, tiles, meta, load_sem, sem, meta_sem,
):
    tile_cols, tile_rows = owner.shape
    tiles_here, levels, _ = adjoint.shape
    lon_count = counts.shape[0]
    me = lax.axis_index("lon")
    asks = [
        pltpu.make_async_copy(whole, here, load_sem.at[n])
        for n, (whole, here) in enumerate(
            ((owner_all, owner), (step_all, step), (column_all, column), (kind_all, kind))
        )
    ]
    for ask in asks:
        ask.start()
    load = pltpu.make_async_copy(adjoint, tiles, load_sem.at[len(asks)])
    load.start()

    for d in range(lon_count):
        counts[d] = 0
        for r in range(CAP):
            codes[d * CAP + r] = 0
    for ask in asks:
        ask.wait()

    def place_rows(n, sent):
        for u in range(4):
            i = n * 4 + u
            for j in range(tile_cols):
                to = owner[j, i]
                rank = counts[to]
                remote = to != me
                counts[to] = rank + 1
                block = (i + step[j, i]) * tile_cols + column[j, i]
                code = block * KINDS + kind[j, i] + 1
                places[i * tile_cols + j] = jnp.where(remote, to * CAP + rank, -code)
                codes[jnp.where(remote, to * CAP + rank, me * CAP)] = jnp.where(remote, code, 0)
                sent = sent + remote.astype(jnp.int32)
        return sent

    sent = lax.fori_loop(0, tile_rows // 4, place_rows, 0)
    load.wait()

    def send_rows(n, carry):
        for u in range(8):
            tile = n * 8 + u
            slot = places[tile]

            @pl.when(slot >= 0)
            def _():
                rows = pl.ds(pl.multiple_of((slot & (CAP - 1)) * levels, levels), levels)
                pltpu.make_async_copy(tiles.at[tile], send.at[slot // CAP, rows, :], sem).start()

        return carry

    lax.fori_loop(0, tiles_here // 8, send_rows, 0)
    lane = lax.broadcasted_iota(jnp.int32, (META, 128), 1)

    def describe(n, carry):
        for u in range(4):
            d = n * 4 + u
            line = jnp.zeros((META, 128), jnp.int32)
            for r in range(CAP):
                code = codes[d * CAP + r]
                line = jnp.where(lane == me * CAP + r, jnp.where(code > EXACT, EXACT - code, code), line)
            meta[d] = line.astype(jnp.float32).astype(jnp.bfloat16)
        return carry

    lax.fori_loop(0, lon_count // 4, describe, 0)
    told = pltpu.make_async_copy(meta, send.at[:, pl.ds(CAP * levels, META), :], meta_sem)
    told.start()

    def settle(_, carry):
        pltpu.make_async_copy(tiles.at[0], send.at[0, pl.ds(0, levels), :], sem).wait()
        return carry

    lax.fori_loop(0, sent, settle, 0)
    told.wait()


def pack(owner, step, column, kind, adjoint, lon_count):
    tiles_here, levels, width = adjoint.shape
    smem = pl.BlockSpec(memory_space=pltpu.SMEM)
    hbm = pl.BlockSpec(memory_space=pltpu.HBM)
    return pl.pallas_call(
        pack_kernel,
        out_shape=(
            pltpu.HBM((lon_count, CAP * levels + META, width), jnp.bfloat16),
            jax.ShapeDtypeStruct((tiles_here,), jnp.int32),
        ),
        in_specs=[hbm] * 5,
        out_specs=(hbm, smem),
        scratch_shapes=[
            pltpu.SMEM(owner.shape, jnp.int32),
            pltpu.SMEM(owner.shape, jnp.int32),
            pltpu.SMEM(owner.shape, jnp.int32),
            pltpu.SMEM(owner.shape, jnp.int32),
            pltpu.SMEM((lon_count * CAP,), jnp.int32),
            pltpu.SMEM((lon_count,), jnp.int32),
            pltpu.VMEM((tiles_here, levels, width), jnp.bfloat16),
            pltpu.VMEM((lon_count, META, width), jnp.bfloat16),
            pltpu.SemaphoreType.DMA((5,)),
            pltpu.SemaphoreType.DMA,
            pltpu.SemaphoreType.DMA,
        ],
        compiler_params=pltpu.CompilerParams(vmem_limit_bytes=60 * 1024 * 1024),
        name="pack",
    )(in_hbm(owner), in_hbm(step), in_hbm(column), in_hbm(kind), in_hbm(adjoint))


def adjoint_kernel(
    places, received, adjoint, old, before, after, blend, east, north,
    result, edge_own, cross_before, cross_after, sensed_remote, sensed_home,
    tiles, sources, sums, remote, home, rounded, edges, back, slopes, listed, codes, work, stay, counts, sem, code_sem, out_sem,
):
    lon_count = received.shape[0]
    tiles_here, levels, width = adjoint.shape
    slot_count = lon_count * CAP
    tile_cols = before.shape[0]
    block_count = tiles_here + 2 * tile_cols
    room = slot_count + UNROLL
    me = lax.axis_index("lon")

    line = received[:, CAP * levels : CAP * levels + META, :].astype(jnp.float32)[:, :8, :]
    code = jnp.sum(line, axis=0).astype(jnp.int32)
    code = jnp.where(code < 0, EXACT - code, code)
    row = lax.broadcasted_iota(jnp.int32, (8, width), 0)
    lane = lax.broadcasted_iota(jnp.int32, (8, width), 1)
    source_device = lane // CAP
    chosen = (code > 0) & (source_device != me) & (((code - 1) & (KINDS - 1)) == row)
    member = chosen.astype(jnp.float32)
    earlier = lax.broadcasted_iota(jnp.int32, (width, width), 0) < lax.broadcasted_iota(jnp.int32, (width, width), 1)
    before_it = jnp.dot(
        member.astype(jnp.bfloat16), earlier.astype(jnp.bfloat16), preferred_element_type=jnp.float32
    ).astype(jnp.int32)
    put_at = jnp.sum(jnp.where(chosen, row * room + before_it + 1, 0), axis=0, keepdims=True)
    put_at = jnp.where(put_at > 0, put_at - 1, KINDS * room)
    total = jnp.sum(member, axis=1, keepdims=True).astype(jnp.int32)
    listed[0:8, :] = jnp.where(row == 0, put_at, jnp.where(row == 1, lane * CODES + code - 1, 0))
    listed[8:16, :] = jnp.broadcast_to(total, (8, width))
    code_copy = pltpu.make_async_copy(listed, codes, code_sem)
    code_copy.start()
    loads = [
        pltpu.make_async_copy(old, sources.at[pl.ds(tile_cols, tiles_here)], sem.at[0]),
        pltpu.make_async_copy(before, sources.at[pl.ds(0, tile_cols)], sem.at[1]),
        pltpu.make_async_copy(after, sources.at[pl.ds(tile_cols + tiles_here, tile_cols)], sem.at[2]),
        pltpu.make_async_copy(adjoint, tiles, sem.at[3]),
    ]
    for copy in loads:
        copy.start()
    for k in range(KINDS):
        back[k] = blend[k].T
        slopes[k, :, :width] = east[k]
        slopes[k, :, width:] = north[k]

    def clear(b, carry):
        sums[b] = jnp.zeros((levels, width), jnp.float32)
        return carry

    lax.fori_loop(0, block_count + 1, clear, 0, unroll=3)

    for k in range(KINDS):
        counts[k] = 0

    def enlist_home(n, carry):
        for u in range(8):
            place = places[n * 8 + u]
            code = -place - 1
            kind = code & (KINDS - 1)
            count = counts[kind]
            stay[kind * room + count] = (n * 8 + u) * CODES + code
            counts[kind] = count + (place < 0).astype(jnp.int32)
        return carry

    lax.fori_loop(0, tiles_here // 8, enlist_home, 0)
    code_copy.wait()
    for slot in range(slot_count):
        work[codes[0, slot]] = codes[1, slot]
    arrived_count = [codes[8 + k, 0] for k in range(KINDS)]
    stay_count = [counts[k] for k in range(KINDS)]
    for k in range(KINDS):
        for u in range(UNROLL):
            work[k * room + arrived_count[k] + u] = slot_count * CODES + block_count * KINDS + k
            stay[k * room + stay_count[k] + u] = tiles_here * CODES + block_count * KINDS + k
    for copy in loads:
        copy.wait()

    def arrived_tile(p):
        p = jnp.minimum(p, slot_count - 1)
        rows = pl.ds(pl.multiple_of((p & (CAP - 1)) * levels, levels), levels)
        return received[p // CAP, rows, :]

    def home_tile(p):
        return tiles[jnp.minimum(p, tiles_here - 1)]

    def some_tiles(kind, entries, tile_at, sensed):
        place = [e // CODES for e in entries]
        block = [(e & (CODES - 1)) // KINDS for e in entries]
        arrived = [tile_at(p) for p in place]
        source = [sources[jnp.minimum(b, block_count - 1)] for b in block]
        spread = jnp.dot(jnp.concatenate(arrived, axis=0), back[kind], preferred_element_type=jnp.float32)
        slope = jnp.dot(jnp.concatenate(source, axis=0), slopes[kind], preferred_element_type=jnp.float32)
        for u in range(UNROLL):
            full = arrived[u].astype(jnp.float32)
            s = slope[u * levels : (u + 1) * levels]
            both = [jnp.sum(full * part, axis=0, keepdims=True) for part in (s[:, :width], s[:, width:])]
            sensed[place[u]] = jnp.concatenate(both, axis=0).astype(sensed.dtype)
        for u in range(UNROLL):
            s = spread[u * levels : (u + 1) * levels]
            sums[block[u]] += s.astype(jnp.bfloat16).astype(jnp.float32)

    for listing, many, tile_at, sensed in (
        (work, arrived_count, arrived_tile, remote),
        (stay, stay_count, home_tile, home),
    ):
        for kind in range(KINDS):

            def step(n, carry, kind=kind, listing=listing, tile_at=tile_at, sensed=sensed):
                entries = [listing[kind * room + n * UNROLL + u] for u in range(UNROLL)]
                some_tiles(kind, entries, tile_at, sensed)
                return carry

            lax.fori_loop(0, (many[kind] + UNROLL - 1) // UNROLL, step, 0)

    copies = []

    def put(source, target):
        copy = pltpu.make_async_copy(source, target, out_sem.at[len(copies)])
        copy.start()
        copies.append(copy)

    put(remote.at[pl.ds(0, slot_count)], sensed_remote)
    put(home.at[pl.ds(0, tiles_here)], sensed_home)
    put(sums.at[pl.ds(tile_cols, tile_cols)], edge_own.at[pl.ds(0, tile_cols)])
    put(sums.at[pl.ds(tiles_here, tile_cols)], edge_own.at[pl.ds(tile_cols, tile_cols)])

    def finish(b, carry):
        rounded[b] = sums[tile_cols + b].astype(jnp.bfloat16)
        return carry

    part = (tiles_here - 2 * tile_cols) // PARTS
    for p in range(PARTS):
        first = tile_cols + p * part
        lax.fori_loop(first, first + part, finish, 0, unroll=3)
        put(rounded.at[pl.ds(first, part)], result.at[pl.ds(first, part)])
    for c in range(tile_cols):
        edges[c] = sums[c].astype(jnp.bfloat16)
        edges[tile_cols + c] = sums[tile_cols + tiles_here + c].astype(jnp.bfloat16)
    put(edges.at[pl.ds(0, tile_cols)], cross_before)
    put(edges.at[pl.ds(tile_cols, tile_cols)], cross_after)
    for copy in copies:
        copy.wait()


def adjoint_step(places, received, adjoint, old, before, after, blend, east, north):
    lon_count = received.shape[0]
    slot_count = lon_count * CAP
    tiles_here, levels, width = adjoint.shape
    tile_cols = before.shape[0]
    block_count = tiles_here + 2 * tile_cols
    assert (block_count + 1) * KINDS <= CODES and block_count * KINDS <= EXACT + 256
    assert slot_count == width and KINDS <= 8 and tiles_here <= slot_count
    smem = pl.BlockSpec(memory_space=pltpu.SMEM)
    vmem = pl.BlockSpec(memory_space=pltpu.VMEM)
    hbm = pl.BlockSpec(memory_space=pltpu.HBM)
    edge = pltpu.HBM((tile_cols, levels, width), jnp.bfloat16)
    return pl.pallas_call(
        adjoint_kernel,
        out_shape=(
            pltpu.HBM((tiles_here, levels, width), jnp.bfloat16),
            pltpu.HBM((2 * tile_cols, levels, width), jnp.float32),
            edge,
            edge,
            pltpu.HBM((slot_count, 2, width), jnp.bfloat16),
            pltpu.HBM((tiles_here, 2, width), jnp.float32),
        ),
        in_specs=[smem, vmem, hbm, hbm, hbm, hbm, vmem, vmem, vmem],
        out_specs=(hbm,) * 6,
        scratch_shapes=[
            pltpu.VMEM((tiles_here, levels, width), jnp.bfloat16),
            pltpu.VMEM((block_count, levels, width), jnp.bfloat16),
            pltpu.VMEM((block_count + 1, levels, width), jnp.float32),
            pltpu.VMEM((slot_count + 1, 2, width), jnp.bfloat16),
            pltpu.VMEM((tiles_here + 1, 2, width), jnp.float32),
            pltpu.VMEM((tiles_here, levels, width), jnp.bfloat16),
            pltpu.VMEM((2 * tile_cols, levels, width), jnp.bfloat16),
            pltpu.VMEM((KINDS, width, width), jnp.bfloat16),
            pltpu.VMEM((KINDS, width, 2 * width), jnp.bfloat16),
            pltpu.VMEM((16, width), jnp.int32),
            pltpu.SMEM((16, width), jnp.int32),
            pltpu.SMEM((KINDS * (slot_count + UNROLL) + 1,), jnp.int32),
            pltpu.SMEM((KINDS * (slot_count + UNROLL),), jnp.int32),
            pltpu.SMEM((KINDS,), jnp.int32),
            pltpu.SemaphoreType.DMA((4,)),
            pltpu.SemaphoreType.DMA,
            pltpu.SemaphoreType.DMA((6 + PARTS,)),
        ],
        compiler_params=pltpu.CompilerParams(vmem_limit_bytes=VMEM_LIMIT),
        name="adjoint",
    )(places, received, in_hbm(adjoint), in_hbm(old), in_hbm(before), in_hbm(after), blend, east, north)


def hold_kernel(edge_own, sensed_home, own, home, sem):
    copies = [
        pltpu.make_async_copy(edge_own, own, sem.at[0]),
        pltpu.make_async_copy(sensed_home, home, sem.at[1]),
    ]
    for copy in copies:
        copy.start()
    for copy in copies:
        copy.wait()


def hold(edge_own, sensed_home):
    vmem = pl.BlockSpec(memory_space=pltpu.VMEM)
    hbm = pl.BlockSpec(memory_space=pltpu.HBM)
    return pl.pallas_call(
        hold_kernel,
        out_shape=(
            pltpu.VMEM(edge_own.shape, edge_own.dtype),
            pltpu.VMEM(sensed_home.shape, sensed_home.dtype),
        ),
        in_specs=[hbm, hbm],
        out_specs=(vmem, vmem),
        scratch_shapes=[pltpu.SemaphoreType.DMA((2,))],
        compiler_params=pltpu.CompilerParams(vmem_limit_bytes=8 * 1024 * 1024),
        name="hold",
    )(in_hbm(edge_own), in_hbm(sensed_home))


def finish_kernel(places, returned, sensed_home, own, from_before, from_after, _, result, sensed, edges, out, sem):
    tiles_here = sensed.shape[0]
    tile_cols = from_before.shape[0]
    for c in range(tile_cols):
        edges[c] = (own[c] + from_before[c].astype(jnp.float32)).astype(jnp.bfloat16)
        edges[tile_cols + c] = (own[tile_cols + c] + from_after[c].astype(jnp.float32)).astype(jnp.bfloat16)
    copies = [
        pltpu.make_async_copy(edges.at[pl.ds(0, tile_cols)], result.at[pl.ds(0, tile_cols)], sem.at[0]),
        pltpu.make_async_copy(
            edges.at[pl.ds(tile_cols, tile_cols)],
            result.at[pl.ds(tiles_here - tile_cols, tile_cols)],
            sem.at[1],
        ),
        pltpu.make_async_copy(out, sensed, sem.at[2]),
    ]
    copies[0].start()
    copies[1].start()

    def place_some(n, carry):
        for u in range(8):
            t = n * 8 + u
            place = places[t]
            out[t] = jnp.where(place < 0, sensed_home[t], returned[jnp.maximum(place, 0)].astype(jnp.float32))
        return carry

    lax.fori_loop(0, tiles_here // 8, place_some, 0)
    copies[2].start()
    for copy in copies:
        copy.wait()


def finish(places, returned, sensed_home, own, from_before, from_after, partial):
    tiles_here, levels, width = partial.shape
    tile_cols = from_before.shape[0]
    smem = pl.BlockSpec(memory_space=pltpu.SMEM)
    vmem = pl.BlockSpec(memory_space=pltpu.VMEM)
    hbm = pl.BlockSpec(memory_space=pltpu.HBM)
    return pl.pallas_call(
        finish_kernel,
        out_shape=(
            pltpu.HBM(partial.shape, partial.dtype),
            pltpu.HBM((tiles_here, 2, width), jnp.float32),
        ),
        in_specs=[smem] + [vmem] * 5 + [hbm],
        out_specs=(hbm, hbm),
        scratch_shapes=[
            pltpu.VMEM((2 * tile_cols, levels, width), jnp.bfloat16),
            pltpu.VMEM((tiles_here, 2, width), jnp.float32),
            pltpu.SemaphoreType.DMA((3,)),
        ],
        input_output_aliases={6: 0},
        compiler_params=pltpu.CompilerParams(vmem_limit_bytes=8 * 1024 * 1024),
        name="finish",
    )(places, in_vmem(returned), in_vmem(sensed_home), in_vmem(own), from_before, from_after, partial)


def on_device(
    tracer_adjoint, tracer_old, owner_lon, row_step, owner_column, tile_kind, blend_weights, slope_east, slope_north
):
    lon_count = lax.axis_size("lon")
    lat_count = lax.axis_size("lat")
    tile_rows, tile_cols = owner_lon.shape
    levels, width = tracer_adjoint.shape[2:]
    tiles_here = tile_rows * tile_cols
    north_to_south = [(i, i + 1) for i in range(lat_count - 1)]
    south_to_north = [(j, i) for i, j in north_to_south]
    adjoint = tracer_adjoint.reshape(tiles_here, levels, width)
    old = tracer_old.reshape(tiles_here, levels, width)

    send, places = pack(owner_lon.T, row_step.T, owner_column.T, tile_kind.T, adjoint, lon_count)
    received = lax.all_to_all(send, "lon", split_axis=0, concat_axis=0, tiled=True)
    before = lax.ppermute(old[-tile_cols:], "lat", north_to_south)
    after = lax.ppermute(old[:tile_cols], "lat", south_to_north)
    partial, edge_own, cross_before, cross_after, sensed_remote, sensed_home = adjoint_step(
        places, received, adjoint, old, before, after, blend_weights, slope_east, slope_north
    )
    returned = lax.all_to_all(sensed_remote, "lon", split_axis=0, concat_axis=0, tiled=True)
    from_after = lax.ppermute(cross_before, "lat", south_to_north)
    from_before = lax.ppermute(cross_after, "lat", north_to_south)
    own, home = hold(edge_own, sensed_home)
    result, sensed = finish(places, returned, home, own, from_before, from_after, partial)
    return (
        result.reshape(tracer_old.shape),
        sensed.reshape(tile_rows, tile_cols, 2, width),
    )


def solution(mesh):
    return jax.shard_map(
        on_device,
        mesh=mesh,
        in_specs=(
            P("lat", "lon", None, None),
            P("lat", "lon", None, None),
            P("lat", "lon"),
            P("lat", "lon"),
            P("lat", "lon"),
            P("lat", "lon"),
            P(),
            P(),
            P(),
        ),
        out_specs=(P("lat", "lon", None, None), P("lat", "lon", None, None)),
        check_vma=False,
    )
```

```python
import functools

import jax
import jax.numpy as jnp
from jax import lax
from jax.experimental import pallas as pl
from jax.experimental.pallas import tpu as pltpu
from jax.sharding import PartitionSpec as P

CAP = 4
META = 16
KINDS = 4
CODES = 512
EXACT = 200
UNROLL = 12
PARTS = 4
VMEM_LIMIT = 24 * 1024 * 1024


def in_hbm(array):
    return pltpu.with_memory_space_constraint(array, pltpu.HBM)


def in_vmem(array):
    return pltpu.with_memory_space_constraint(array, pltpu.VMEM)


def pack_kernel(
    owner_all, step_all, column_all, kind_all, adjoint, send, places,
    owner, step, column, kind, codes, counts, tiles, meta, load_sem, sem, meta_sem,
):
    tile_cols, tile_rows = owner.shape
    tiles_here, levels, _ = adjoint.shape
    lon_count = counts.shape[0]
    me = lax.axis_index("lon")
    asks = [
        pltpu.make_async_copy(whole, here, load_sem.at[n])
        for n, (whole, here) in enumerate(
            ((owner_all, owner), (step_all, step), (column_all, column), (kind_all, kind))
        )
    ]
    for ask in asks:
        ask.start()
    load = pltpu.make_async_copy(adjoint, tiles, load_sem.at[len(asks)])
    load.start()

    for d in range(lon_count):
        counts[d] = 0
        for r in range(CAP):
            codes[d * CAP + r] = 0
    for ask in asks:
        ask.wait()
    load.wait()

    def send_rows(n, sent):
        for u in range(4):
            i = n * 4 + u
            for j in range(tile_cols):
                tile = i * tile_cols + j
                to = owner[j, i]
                rank = counts[to]
                remote = to != me
                counts[to] = rank + 1
                code = ((i + step[j, i]) * tile_cols + column[j, i]) * KINDS + kind[j, i] + 1
                slot = to * CAP + rank
                places[tile] = jnp.where(remote, slot, -code)
                codes[jnp.where(remote, slot, me * CAP)] = jnp.where(remote, code, 0)

                @pl.when(remote)
                def _():
                    rows = pl.ds(pl.multiple_of(rank * levels, levels), levels)
                    pltpu.make_async_copy(tiles.at[tile], send.at[to, rows, :], sem).start()

                sent = sent + remote.astype(jnp.int32)
        return sent

    sent = lax.fori_loop(0, tile_rows // 4, send_rows, 0)
    lane = lax.broadcasted_iota(jnp.int32, (8, meta.shape[2]), 1)
    lines = [jnp.zeros(lane.shape, jnp.int32)] * CAP
    for d in range(lon_count):
        for r in range(CAP):
            lines[r] = jnp.where(lane == d * CAP + r, codes[d * CAP + r], lines[r])
    line = sum(lines[1:], lines[0])
    line = jnp.where(line > EXACT, EXACT - line, line).astype(jnp.float32)
    line = jnp.concatenate([line, line], axis=0).astype(jnp.bfloat16)
    for d in range(lon_count):
        meta[d] = line
    told = pltpu.make_async_copy(meta, send.at[:, pl.ds(CAP * levels, META), :], meta_sem)
    told.start()

    def settle(_, carry):
        pltpu.make_async_copy(tiles.at[0], send.at[0, pl.ds(0, levels), :], sem).wait()
        return carry

    lax.fori_loop(0, sent, settle, 0)
    told.wait()


def pack(owner, step, column, kind, adjoint, lon_count):
    tiles_here, levels, width = adjoint.shape
    smem = pl.BlockSpec(memory_space=pltpu.SMEM)
    hbm = pl.BlockSpec(memory_space=pltpu.HBM)
    return pl.pallas_call(
        pack_kernel,
        out_shape=(
            pltpu.HBM((lon_count, CAP * levels + META, width), jnp.bfloat16),
            jax.ShapeDtypeStruct((tiles_here,), jnp.int32),
        ),
        in_specs=[hbm] * 5,
        out_specs=(hbm, smem),
        scratch_shapes=[
            pltpu.SMEM(owner.shape, jnp.int32),
            pltpu.SMEM(owner.shape, jnp.int32),
            pltpu.SMEM(owner.shape, jnp.int32),
            pltpu.SMEM(owner.shape, jnp.int32),
            pltpu.SMEM((lon_count * CAP,), jnp.int32),
            pltpu.SMEM((lon_count,), jnp.int32),
            pltpu.VMEM((tiles_here, levels, width), jnp.bfloat16),
            pltpu.VMEM((lon_count, META, width), jnp.bfloat16),
            pltpu.SemaphoreType.DMA((5,)),
            pltpu.SemaphoreType.DMA,
            pltpu.SemaphoreType.DMA,
        ],
        compiler_params=pltpu.CompilerParams(vmem_limit_bytes=60 * 1024 * 1024),
        name="pack",
    )(in_hbm(owner), in_hbm(step), in_hbm(column), in_hbm(kind), in_hbm(adjoint))


def adjoint_kernel(
    places_all, received, adjoint, old, before, after, blend_all, east_all, north_all,
    result, edge_own, cross_before, cross_after, sensed_remote, sensed_home,
    tiles, sources, sums, remote, home, rounded, edges, blend, back, slopes, listed, places, codes, work, stay, counts, sem, code_sem, out_sem,
):
    lon_count = received.shape[0]
    tiles_here, levels, width = adjoint.shape
    slot_count = lon_count * CAP
    tile_cols = before.shape[0]
    block_count = tiles_here + 2 * tile_cols
    room = slot_count + UNROLL
    me = lax.axis_index("lon")

    told = received[:, CAP * levels : CAP * levels + META, :].astype(jnp.float32)[:, 0, :]
    device = lax.broadcasted_iota(jnp.int32, (lon_count, width), 0)
    spot = lax.broadcasted_iota(jnp.int32, (lon_count, width), 1)
    told = jnp.where(spot // CAP == me, told, 0.0).astype(jnp.bfloat16)
    first = lax.broadcasted_iota(jnp.int32, (width, width), 0)
    second = lax.broadcasted_iota(jnp.int32, (width, width), 1)
    again = ((first - second) % CAP == 0).astype(jnp.bfloat16)
    asked = jnp.dot(told, again, preferred_element_type=jnp.float32)
    code = jnp.sum(jnp.where(spot // CAP == device, asked, 0.0), axis=0, keepdims=True).astype(jnp.int32)
    code = jnp.where(code < 0, EXACT - code, code)
    row = lax.broadcasted_iota(jnp.int32, (8, width), 0)
    lane = lax.broadcasted_iota(jnp.int32, (8, width), 1)
    source_device = lane // CAP
    chosen = (code > 0) & (source_device != me) & (((code - 1) & (KINDS - 1)) == row)
    member = chosen.astype(jnp.float32)
    earlier = first < second
    before_it = jnp.dot(
        member.astype(jnp.bfloat16), earlier.astype(jnp.bfloat16), preferred_element_type=jnp.float32
    ).astype(jnp.int32)
    put_at = jnp.sum(jnp.where(chosen, row * room + before_it + 1, 0), axis=0, keepdims=True)
    put_at = jnp.where(put_at > 0, put_at - 1, KINDS * room)
    total = jnp.sum(member, axis=1, keepdims=True).astype(jnp.int32)
    listed[0:8, :] = jnp.where(row == 0, put_at, jnp.where(row == 1, lane * CODES + code - 1, 0))
    listed[8:16, :] = jnp.broadcast_to(total, (8, width))
    code_copy = pltpu.make_async_copy(listed, codes, code_sem)
    code_copy.start()
    loads = [
        pltpu.make_async_copy(old, sources.at[pl.ds(tile_cols, tiles_here)], sem.at[0]),
        pltpu.make_async_copy(before, sources.at[pl.ds(0, tile_cols)], sem.at[1]),
        pltpu.make_async_copy(after, sources.at[pl.ds(tile_cols + tiles_here, tile_cols)], sem.at[2]),
        pltpu.make_async_copy(adjoint, tiles, sem.at[3]),
    ]
    weights = [
        pltpu.make_async_copy(blend_all, blend, sem.at[4]),
        pltpu.make_async_copy(east_all, slopes.at[:, :, pl.ds(0, width)], sem.at[5]),
        pltpu.make_async_copy(north_all, slopes.at[:, :, pl.ds(width, width)], sem.at[6]),
        pltpu.make_async_copy(places_all, places, sem.at[7]),
    ]
    for copy in weights:
        copy.start()
    for copy in loads:
        copy.start()
    def clear(b, carry):
        sums[b] = jnp.zeros((levels, width), jnp.float32)
        return carry

    lax.fori_loop(0, block_count + 1, clear, 0, unroll=3)

    for copy in weights:
        copy.wait()
    for k in range(KINDS):
        back[k] = blend[k].T

    for k in range(KINDS):
        counts[k] = 0

    def enlist_home(n, carry):
        for u in range(8):
            place = places[n * 8 + u]
            code = -place - 1
            kind = code & (KINDS - 1)
            count = counts[kind]
            stay[kind * room + count] = (n * 8 + u) * CODES + code
            counts[kind] = count + (place < 0).astype(jnp.int32)
        return carry

    lax.fori_loop(0, tiles_here // 8, enlist_home, 0)
    code_copy.wait()
    for slot in range(slot_count):
        work[codes[0, slot]] = codes[1, slot]
    arrived_count = [codes[8 + k, 0] for k in range(KINDS)]
    stay_count = [counts[k] for k in range(KINDS)]
    for k in range(KINDS):
        for u in range(UNROLL):
            work[k * room + arrived_count[k] + u] = slot_count * CODES + block_count * KINDS + k
            stay[k * room + stay_count[k] + u] = tiles_here * CODES + block_count * KINDS + k
    for copy in loads[:3]:
        copy.wait()

    def arrived_tile(p):
        p = jnp.minimum(p, slot_count - 1)
        rows = pl.ds(pl.multiple_of((p & (CAP - 1)) * levels, levels), levels)
        return received[p // CAP, rows, :]

    def home_tile(p):
        return tiles[jnp.minimum(p, tiles_here - 1)]

    def some_tiles(kind, entries, tile_at, sensed):
        place = [e // CODES for e in entries]
        block = [(e & (CODES - 1)) // KINDS for e in entries]
        arrived = [tile_at(p) for p in place]
        source = [sources[jnp.minimum(b, block_count - 1)] for b in block]
        spread = jnp.dot(jnp.concatenate(arrived, axis=0), back[kind], preferred_element_type=jnp.float32)
        slope = jnp.dot(jnp.concatenate(source, axis=0), slopes[kind], preferred_element_type=jnp.float32)
        for u in range(UNROLL):
            full = arrived[u].astype(jnp.float32)
            s = slope[u * levels : (u + 1) * levels]
            both = [jnp.sum(full * part, axis=0, keepdims=True) for part in (s[:, :width], s[:, width:])]
            sensed[place[u]] = jnp.concatenate(both, axis=0).astype(sensed.dtype)
        for u in range(UNROLL):
            s = spread[u * levels : (u + 1) * levels]
            sums[block[u]] += s.astype(jnp.bfloat16).astype(jnp.float32)

    for where, (listing, many, tile_at, sensed) in enumerate((
        (work, arrived_count, arrived_tile, remote),
        (stay, stay_count, home_tile, home),
    )):
        if where == 1:
            loads[3].wait()
        for kind in range(KINDS):

            def step(n, carry, kind=kind, listing=listing, tile_at=tile_at, sensed=sensed):
                entries = [listing[kind * room + n * UNROLL + u] for u in range(UNROLL)]
                some_tiles(kind, entries, tile_at, sensed)
                return carry

            lax.fori_loop(0, (many[kind] + UNROLL - 1) // UNROLL, step, 0)

    copies = []

    def put(source, target):
        copy = pltpu.make_async_copy(source, target, out_sem.at[len(copies)])
        copy.start()
        copies.append(copy)

    put(remote.at[pl.ds(0, slot_count)], sensed_remote)
    put(home.at[pl.ds(0, tiles_here)], sensed_home)
    put(sums.at[pl.ds(tile_cols, tile_cols)], edge_own.at[pl.ds(0, tile_cols)])
    put(sums.at[pl.ds(tiles_here, tile_cols)], edge_own.at[pl.ds(tile_cols, tile_cols)])

    def finish(b, carry):
        rounded[b] = sums[tile_cols + b].astype(jnp.bfloat16)
        return carry

    part = (tiles_here - 2 * tile_cols) // PARTS
    for p in range(PARTS):
        first = tile_cols + p * part
        lax.fori_loop(first, first + part, finish, 0, unroll=3)
        put(rounded.at[pl.ds(first, part)], result.at[pl.ds(first, part)])
    for c in range(tile_cols):
        edges[c] = sums[c].astype(jnp.bfloat16)
        edges[tile_cols + c] = sums[tile_cols + tiles_here + c].astype(jnp.bfloat16)
    put(edges.at[pl.ds(0, tile_cols)], cross_before)
    put(edges.at[pl.ds(tile_cols, tile_cols)], cross_after)
    for copy in copies:
        copy.wait()


def adjoint_step(places, received, adjoint, old, before, after, blend, east, north):
    lon_count = received.shape[0]
    slot_count = lon_count * CAP
    tiles_here, levels, width = adjoint.shape
    tile_cols = before.shape[0]
    block_count = tiles_here + 2 * tile_cols
    assert (block_count + 1) * KINDS <= CODES and block_count * KINDS <= EXACT + 256
    assert slot_count == width and KINDS <= 8 and tiles_here <= slot_count
    vmem = pl.BlockSpec(memory_space=pltpu.VMEM)
    hbm = pl.BlockSpec(memory_space=pltpu.HBM)
    edge = pltpu.HBM((tile_cols, levels, width), jnp.bfloat16)
    return pl.pallas_call(
        adjoint_kernel,
        out_shape=(
            pltpu.HBM((tiles_here, levels, width), jnp.bfloat16),
            pltpu.HBM((2 * tile_cols, levels, width), jnp.float32),
            edge,
            edge,
            pltpu.HBM((slot_count, 2, width), jnp.bfloat16),
            pltpu.HBM((tiles_here, 2, width), jnp.float32),
        ),
        in_specs=[hbm, vmem] + [hbm] * 7,
        out_specs=(hbm,) * 6,
        scratch_shapes=[
            pltpu.VMEM((tiles_here, levels, width), jnp.bfloat16),
            pltpu.VMEM((block_count, levels, width), jnp.bfloat16),
            pltpu.VMEM((block_count + 1, levels, width), jnp.float32),
            pltpu.VMEM((slot_count + 1, 2, width), jnp.bfloat16),
            pltpu.VMEM((tiles_here + 1, 2, width), jnp.float32),
            pltpu.VMEM((tiles_here, levels, width), jnp.bfloat16),
            pltpu.VMEM((2 * tile_cols, levels, width), jnp.bfloat16),
            pltpu.VMEM((KINDS, width, width), jnp.bfloat16),
            pltpu.VMEM((KINDS, width, width), jnp.bfloat16),
            pltpu.VMEM((KINDS, width, 2 * width), jnp.bfloat16),
            pltpu.VMEM((16, width), jnp.int32),
            pltpu.SMEM((tiles_here,), jnp.int32),
            pltpu.SMEM((16, width), jnp.int32),
            pltpu.SMEM((KINDS * (slot_count + UNROLL) + 1,), jnp.int32),
            pltpu.SMEM((KINDS * (slot_count + UNROLL),), jnp.int32),
            pltpu.SMEM((KINDS,), jnp.int32),
            pltpu.SemaphoreType.DMA((8,)),
            pltpu.SemaphoreType.DMA,
            pltpu.SemaphoreType.DMA((6 + PARTS,)),
        ],
        compiler_params=pltpu.CompilerParams(vmem_limit_bytes=VMEM_LIMIT),
        name="adjoint",
    )(
        in_hbm(places), received, in_hbm(adjoint), in_hbm(old), in_hbm(before), in_hbm(after),
        in_hbm(blend), in_hbm(east), in_hbm(north),
    )


def hold_kernel(edge_own, sensed_home, own, home, sem):
    copies = [
        pltpu.make_async_copy(edge_own, own, sem.at[0]),
        pltpu.make_async_copy(sensed_home, home, sem.at[1]),
    ]
    for copy in copies:
        copy.start()
    for copy in copies:
        copy.wait()


def hold(edge_own, sensed_home):
    vmem = pl.BlockSpec(memory_space=pltpu.VMEM)
    hbm = pl.BlockSpec(memory_space=pltpu.HBM)
    return pl.pallas_call(
        hold_kernel,
        out_shape=(
            pltpu.VMEM(edge_own.shape, edge_own.dtype),
            pltpu.VMEM(sensed_home.shape, sensed_home.dtype),
        ),
        in_specs=[hbm, hbm],
        out_specs=(vmem, vmem),
        scratch_shapes=[pltpu.SemaphoreType.DMA((2,))],
        compiler_params=pltpu.CompilerParams(vmem_limit_bytes=8 * 1024 * 1024),
        name="hold",
    )(in_hbm(edge_own), in_hbm(sensed_home))


def finish_kernel(
    places_all, returned, sensed_home, own, from_before, from_after, _, result, sensed, edges, out, places, sem
):
    where = pltpu.make_async_copy(places_all, places, sem.at[3])
    where.start()
    tiles_here = sensed.shape[0]
    tile_cols = from_before.shape[0]
    for c in range(tile_cols):
        edges[c] = (own[c] + from_before[c].astype(jnp.float32)).astype(jnp.bfloat16)
        edges[tile_cols + c] = (own[tile_cols + c] + from_after[c].astype(jnp.float32)).astype(jnp.bfloat16)
    copies = [
        pltpu.make_async_copy(edges.at[pl.ds(0, tile_cols)], result.at[pl.ds(0, tile_cols)], sem.at[0]),
        pltpu.make_async_copy(
            edges.at[pl.ds(tile_cols, tile_cols)],
            result.at[pl.ds(tiles_here - tile_cols, tile_cols)],
            sem.at[1],
        ),
        pltpu.make_async_copy(out, sensed, sem.at[2]),
    ]
    copies[0].start()
    copies[1].start()
    where.wait()

    def place_some(n, carry):
        for u in range(8):
            t = n * 8 + u
            place = places[t]
            out[t] = jnp.where(place < 0, sensed_home[t], returned[jnp.maximum(place, 0)].astype(jnp.float32))
        return carry

    lax.fori_loop(0, tiles_here // 8, place_some, 0)
    copies[2].start()
    for copy in copies:
        copy.wait()


def finish(places, returned, sensed_home, own, from_before, from_after, partial):
    tiles_here, levels, width = partial.shape
    tile_cols = from_before.shape[0]
    vmem = pl.BlockSpec(memory_space=pltpu.VMEM)
    hbm = pl.BlockSpec(memory_space=pltpu.HBM)
    return pl.pallas_call(
        finish_kernel,
        out_shape=(
            pltpu.HBM(partial.shape, partial.dtype),
            pltpu.HBM((tiles_here, 2, width), jnp.float32),
        ),
        in_specs=[hbm] + [vmem] * 5 + [hbm],
        out_specs=(hbm, hbm),
        scratch_shapes=[
            pltpu.VMEM((2 * tile_cols, levels, width), jnp.bfloat16),
            pltpu.VMEM((tiles_here, 2, width), jnp.float32),
            pltpu.SMEM((tiles_here,), jnp.int32),
            pltpu.SemaphoreType.DMA((4,)),
        ],
        input_output_aliases={6: 0},
        compiler_params=pltpu.CompilerParams(vmem_limit_bytes=8 * 1024 * 1024),
        name="finish",
    )(in_hbm(places), in_vmem(returned), in_vmem(sensed_home), in_vmem(own), from_before, from_after, partial)


def on_device(
    tracer_adjoint, tracer_old, owner_lon, row_step, owner_column, tile_kind, blend_weights, slope_east, slope_north
):
    lon_count = lax.axis_size("lon")
    lat_count = lax.axis_size("lat")
    tile_rows, tile_cols = owner_lon.shape
    levels, width = tracer_adjoint.shape[2:]
    tiles_here = tile_rows * tile_cols
    north_to_south = [(i, i + 1) for i in range(lat_count - 1)]
    south_to_north = [(j, i) for i, j in north_to_south]
    adjoint = tracer_adjoint.reshape(tiles_here, levels, width)
    old = tracer_old.reshape(tiles_here, levels, width)

    send, places = pack(owner_lon.T, row_step.T, owner_column.T, tile_kind.T, adjoint, lon_count)
    received = lax.all_to_all(send, "lon", split_axis=0, concat_axis=0, tiled=True)
    before = lax.ppermute(old[-tile_cols:], "lat", north_to_south)
    after = lax.ppermute(old[:tile_cols], "lat", south_to_north)
    partial, edge_own, cross_before, cross_after, sensed_remote, sensed_home = adjoint_step(
        places, received, adjoint, old, before, after, blend_weights, slope_east, slope_north
    )
    returned = lax.all_to_all(sensed_remote, "lon", split_axis=0, concat_axis=0, tiled=True)
    from_after = lax.ppermute(cross_before, "lat", south_to_north)
    from_before = lax.ppermute(cross_after, "lat", north_to_south)
    own, home = hold(edge_own, sensed_home)
    result, sensed = finish(places, returned, home, own, from_before, from_after, partial)
    return (
        result.reshape(tracer_old.shape),
        sensed.reshape(tile_rows, tile_cols, 2, width),
    )


def solution(mesh):
    return jax.shard_map(
        on_device,
        mesh=mesh,
        in_specs=(
            P("lat", "lon", None, None),
            P("lat", "lon", None, None),
            P("lat", "lon"),
            P("lat", "lon"),
            P("lat", "lon"),
            P("lat", "lon"),
            P(),
            P(),
            P(),
        ),
        out_specs=(P("lat", "lon", None, None), P("lat", "lon", None, None)),
        check_vma=False,
    )
```

```python
import functools

import jax
import jax.numpy as jnp
from jax import lax
from jax.experimental import pallas as pl
from jax.experimental.pallas import tpu as pltpu
from jax.sharding import PartitionSpec as P

CAP = 4
META = 16
KINDS = 4
CODES = 512
EXACT = 200
UNROLL = 12
PARTS = 4
VMEM_LIMIT = 24 * 1024 * 1024


def in_hbm(array):
    return pltpu.with_memory_space_constraint(array, pltpu.HBM)


def in_vmem(array):
    return pltpu.with_memory_space_constraint(array, pltpu.VMEM)


def pack_kernel(
    owner_all, step_all, column_all, kind_all, adjoint, send, places,
    owner, step, column, kind, counts, rows, tiles, meta, list_sem, load_sem, sem, meta_sem,
):
    tile_cols, tile_rows = owner.shape
    tiles_here, levels, _ = adjoint.shape
    lon_count = counts.shape[0]
    me = lax.axis_index("lon")
    wholes = (owner_all, step_all, column_all, kind_all)
    lists = [
        pltpu.make_async_copy(whole, rows.at[n], list_sem.at[n]) for n, whole in enumerate(wholes)
    ]
    asks = [
        pltpu.make_async_copy(whole, here, load_sem.at[n])
        for n, (whole, here) in enumerate(zip(wholes, (owner, step, column, kind)))
    ]
    for ask in lists + asks:
        ask.start()
    load = pltpu.make_async_copy(adjoint, tiles, load_sem.at[len(asks)])
    load.start()

    for d in range(lon_count):
        counts[d] = 0
    for ask in lists:
        ask.wait()

    wide = (lon_count, tile_rows)
    device = lax.broadcasted_iota(jnp.int32, wide, 0)
    named, asked = [], []
    for j in range(tile_cols):
        to = jnp.broadcast_to(rows[0, j : j + 1, :], wide)
        block = (lax.broadcasted_iota(jnp.int32, (1, tile_rows), 1) + rows[1, j : j + 1, :]) * tile_cols
        code = (block + rows[2, j : j + 1, :]) * KINDS + rows[3, j : j + 1, :] + 1
        named.append((to == device) & (to != me))
        asked.append(jnp.broadcast_to(code, wide))
    square = (tile_rows, tile_rows)
    earlier = lax.broadcasted_iota(jnp.int32, square, 0) < lax.broadcasted_iota(jnp.int32, square, 1)
    in_row = sum(n.astype(jnp.float32) for n in named)
    rank = jnp.dot(
        in_row.astype(jnp.bfloat16), earlier.astype(jnp.bfloat16), preferred_element_type=jnp.float32
    ).astype(jnp.int32)
    lane = lax.broadcasted_iota(jnp.int32, (lon_count, meta.shape[2]), 1)
    spread = jnp.zeros(lane.shape, jnp.float32)
    ranks = []
    for j in range(tile_cols):
        ranks.append(rank)
        rank = rank + named[j].astype(jnp.int32)
    for r in range(CAP):
        of_rank = sum(
            jnp.where(named[j] & (ranks[j] == r), asked[j], 0).astype(jnp.float32) for j in range(tile_cols)
        )
        of_rank = jnp.sum(of_rank, axis=1, keepdims=True)
        spread = jnp.where(lane % CAP == r, of_rank, spread)
    mine = lane // CAP == lax.broadcasted_iota(jnp.int32, lane.shape, 0)
    line = jnp.sum(jnp.where(mine, spread, 0.0), axis=0, keepdims=True)
    line = jnp.where(line > EXACT, EXACT - line, line)
    line = jnp.broadcast_to(line, (META, meta.shape[2])).astype(jnp.bfloat16)
    for d in range(lon_count):
        meta[d] = line
    told = pltpu.make_async_copy(meta, send.at[:, pl.ds(CAP * levels, META), :], meta_sem)
    told.start()
    for ask in asks:
        ask.wait()
    load.wait()

    def send_rows(n, sent):
        for u in range(4):
            i = n * 4 + u
            for j in range(tile_cols):
                tile = i * tile_cols + j
                to = owner[j, i]
                rank = counts[to]
                remote = to != me
                counts[to] = rank + 1
                code = ((i + step[j, i]) * tile_cols + column[j, i]) * KINDS + kind[j, i] + 1
                slot = to * CAP + rank
                places[tile] = jnp.where(remote, slot, -code)

                @pl.when(remote)
                def _():
                    rows = pl.ds(pl.multiple_of(rank * levels, levels), levels)
                    pltpu.make_async_copy(tiles.at[tile], send.at[to, rows, :], sem).start()

                sent = sent + remote.astype(jnp.int32)
        return sent

    sent = lax.fori_loop(0, tile_rows // 4, send_rows, 0)
    def settle(_, carry):
        pltpu.make_async_copy(tiles.at[0], send.at[0, pl.ds(0, levels), :], sem).wait()
        return carry

    lax.fori_loop(0, sent, settle, 0)
    told.wait()


def pack(owner, step, column, kind, adjoint, lon_count):
    tiles_here, levels, width = adjoint.shape
    smem = pl.BlockSpec(memory_space=pltpu.SMEM)
    hbm = pl.BlockSpec(memory_space=pltpu.HBM)
    return pl.pallas_call(
        pack_kernel,
        out_shape=(
            pltpu.HBM((lon_count, CAP * levels + META, width), jnp.bfloat16),
            jax.ShapeDtypeStruct((tiles_here,), jnp.int32),
        ),
        in_specs=[hbm] * 5,
        out_specs=(hbm, smem),
        scratch_shapes=[
            pltpu.SMEM(owner.shape, jnp.int32),
            pltpu.SMEM(owner.shape, jnp.int32),
            pltpu.SMEM(owner.shape, jnp.int32),
            pltpu.SMEM(owner.shape, jnp.int32),
            pltpu.SMEM((lon_count,), jnp.int32),
            pltpu.VMEM((4,) + owner.shape, jnp.int32),
            pltpu.VMEM((tiles_here, levels, width), jnp.bfloat16),
            pltpu.VMEM((lon_count, META, width), jnp.bfloat16),
            pltpu.SemaphoreType.DMA((4,)),
            pltpu.SemaphoreType.DMA((5,)),
            pltpu.SemaphoreType.DMA,
            pltpu.SemaphoreType.DMA,
        ],
        compiler_params=pltpu.CompilerParams(vmem_limit_bytes=60 * 1024 * 1024),
        name="pack",
    )(in_hbm(owner), in_hbm(step), in_hbm(column), in_hbm(kind), in_hbm(adjoint))


def adjoint_kernel(
    places_all, received, adjoint, old, before, after, blend_all, east_all, north_all,
    result, edge_own, cross_before, cross_after, sensed_remote, sensed_home,
    tiles, sources, sums, remote, home, rounded, edges, blend, back, slopes, listed, places, codes, work, stay, counts, sem, code_sem, out_sem,
):
    lon_count = received.shape[0]
    tiles_here, levels, width = adjoint.shape
    slot_count = lon_count * CAP
    tile_cols = before.shape[0]
    block_count = tiles_here + 2 * tile_cols
    room = slot_count + UNROLL
    me = lax.axis_index("lon")

    told = received[:, CAP * levels : CAP * levels + META, :].astype(jnp.float32)[:, 0, :]
    device = lax.broadcasted_iota(jnp.int32, (lon_count, width), 0)
    spot = lax.broadcasted_iota(jnp.int32, (lon_count, width), 1)
    told = jnp.where(spot // CAP == me, told, 0.0).astype(jnp.bfloat16)
    first = lax.broadcasted_iota(jnp.int32, (width, width), 0)
    second = lax.broadcasted_iota(jnp.int32, (width, width), 1)
    again = ((first - second) % CAP == 0).astype(jnp.bfloat16)
    asked = jnp.dot(told, again, preferred_element_type=jnp.float32)
    code = jnp.sum(jnp.where(spot // CAP == device, asked, 0.0), axis=0, keepdims=True).astype(jnp.int32)
    code = jnp.where(code < 0, EXACT - code, code)
    row = lax.broadcasted_iota(jnp.int32, (8, width), 0)
    lane = lax.broadcasted_iota(jnp.int32, (8, width), 1)
    source_device = lane // CAP
    chosen = (code > 0) & (source_device != me) & (((code - 1) & (KINDS - 1)) == row)
    member = chosen.astype(jnp.float32)
    earlier = first < second
    before_it = jnp.dot(
        member.astype(jnp.bfloat16), earlier.astype(jnp.bfloat16), preferred_element_type=jnp.float32
    ).astype(jnp.int32)
    put_at = jnp.sum(jnp.where(chosen, row * room + before_it + 1, 0), axis=0, keepdims=True)
    put_at = jnp.where(put_at > 0, put_at - 1, KINDS * room)
    total = jnp.sum(member, axis=1, keepdims=True).astype(jnp.int32)
    listed[0:8, :] = jnp.where(row == 0, put_at, jnp.where(row == 1, lane * CODES + code - 1, 0))
    listed[8:16, :] = jnp.broadcast_to(total, (8, width))
    code_copy = pltpu.make_async_copy(listed, codes, code_sem)
    code_copy.start()
    loads = [
        pltpu.make_async_copy(old, sources.at[pl.ds(tile_cols, tiles_here)], sem.at[0]),
        pltpu.make_async_copy(before, sources.at[pl.ds(0, tile_cols)], sem.at[1]),
        pltpu.make_async_copy(after, sources.at[pl.ds(tile_cols + tiles_here, tile_cols)], sem.at[2]),
        pltpu.make_async_copy(adjoint, tiles, sem.at[3]),
    ]
    weights = [
        pltpu.make_async_copy(blend_all, blend, sem.at[4]),
        pltpu.make_async_copy(east_all, slopes.at[:, :, pl.ds(0, width)], sem.at[5]),
        pltpu.make_async_copy(north_all, slopes.at[:, :, pl.ds(width, width)], sem.at[6]),
        pltpu.make_async_copy(places_all, places, sem.at[7]),
    ]
    for copy in weights:
        copy.start()
    for copy in loads:
        copy.start()
    def clear(b, carry):
        sums[b] = jnp.zeros((levels, width), jnp.float32)
        return carry

    lax.fori_loop(0, block_count + 1, clear, 0, unroll=3)

    for copy in weights:
        copy.wait()
    for k in range(KINDS):
        back[k] = blend[k].T

    for k in range(KINDS):
        counts[k] = 0

    def enlist_home(n, carry):
        for u in range(8):
            place = places[n * 8 + u]
            code = -place - 1
            kind = code & (KINDS - 1)
            count = counts[kind]
            stay[kind * room + count] = (n * 8 + u) * CODES + code
            counts[kind] = count + (place < 0).astype(jnp.int32)
        return carry

    lax.fori_loop(0, tiles_here // 8, enlist_home, 0)
    code_copy.wait()
    for slot in range(slot_count):
        work[codes[0, slot]] = codes[1, slot]
    arrived_count = [codes[8 + k, 0] for k in range(KINDS)]
    stay_count = [counts[k] for k in range(KINDS)]
    for k in range(KINDS):
        for u in range(UNROLL):
            work[k * room + arrived_count[k] + u] = slot_count * CODES + block_count * KINDS + k
            stay[k * room + stay_count[k] + u] = tiles_here * CODES + block_count * KINDS + k
    for copy in loads[:3]:
        copy.wait()

    def arrived_tile(p):
        p = jnp.minimum(p, slot_count - 1)
        rows = pl.ds(pl.multiple_of((p & (CAP - 1)) * levels, levels), levels)
        return received[p // CAP, rows, :]

    def home_tile(p):
        return tiles[jnp.minimum(p, tiles_here - 1)]

    def some_tiles(kind, entries, tile_at, sensed):
        place = [e // CODES for e in entries]
        block = [(e & (CODES - 1)) // KINDS for e in entries]
        arrived = [tile_at(p) for p in place]
        source = [sources[jnp.minimum(b, block_count - 1)] for b in block]
        spread = jnp.dot(jnp.concatenate(arrived, axis=0), back[kind], preferred_element_type=jnp.float32)
        slope = jnp.dot(jnp.concatenate(source, axis=0), slopes[kind], preferred_element_type=jnp.float32)
        for u in range(UNROLL):
            full = arrived[u].astype(jnp.float32)
            s = slope[u * levels : (u + 1) * levels]
            both = [jnp.sum(full * part, axis=0, keepdims=True) for part in (s[:, :width], s[:, width:])]
            sensed[place[u]] = jnp.concatenate(both, axis=0).astype(sensed.dtype)
        for u in range(UNROLL):
            s = spread[u * levels : (u + 1) * levels]
            sums[block[u]] += s.astype(jnp.bfloat16).astype(jnp.float32)

    for where, (listing, many, tile_at, sensed) in enumerate((
        (work, arrived_count, arrived_tile, remote),
        (stay, stay_count, home_tile, home),
    )):
        if where == 1:
            loads[3].wait()
        for kind in range(KINDS):

            def step(n, carry, kind=kind, listing=listing, tile_at=tile_at, sensed=sensed):
                entries = [listing[kind * room + n * UNROLL + u] for u in range(UNROLL)]
                some_tiles(kind, entries, tile_at, sensed)
                return carry

            lax.fori_loop(0, (many[kind] + UNROLL - 1) // UNROLL, step, 0)

    copies = []

    def put(source, target):
        copy = pltpu.make_async_copy(source, target, out_sem.at[len(copies)])
        copy.start()
        copies.append(copy)

    put(remote.at[pl.ds(0, slot_count)], sensed_remote)
    put(home.at[pl.ds(0, tiles_here)], sensed_home)
    put(sums.at[pl.ds(tile_cols, tile_cols)], edge_own.at[pl.ds(0, tile_cols)])
    put(sums.at[pl.ds(tiles_here, tile_cols)], edge_own.at[pl.ds(tile_cols, tile_cols)])

    def finish(b, carry):
        rounded[b] = sums[tile_cols + b].astype(jnp.bfloat16)
        return carry

    part = (tiles_here - 2 * tile_cols) // PARTS
    for p in range(PARTS):
        first = tile_cols + p * part
        lax.fori_loop(first, first + part, finish, 0, unroll=3)
        put(rounded.at[pl.ds(first, part)], result.at[pl.ds(first, part)])
    for c in range(tile_cols):
        edges[c] = sums[c].astype(jnp.bfloat16)
        edges[tile_cols + c] = sums[tile_cols + tiles_here + c].astype(jnp.bfloat16)
    put(edges.at[pl.ds(0, tile_cols)], cross_before)
    put(edges.at[pl.ds(tile_cols, tile_cols)], cross_after)
    for copy in copies:
        copy.wait()


def adjoint_step(places, received, adjoint, old, before, after, blend, east, north):
    lon_count = received.shape[0]
    slot_count = lon_count * CAP
    tiles_here, levels, width = adjoint.shape
    tile_cols = before.shape[0]
    block_count = tiles_here + 2 * tile_cols
    assert (block_count + 1) * KINDS <= CODES and block_count * KINDS <= EXACT + 256
    assert slot_count == width and KINDS <= 8 and tiles_here <= slot_count
    vmem = pl.BlockSpec(memory_space=pltpu.VMEM)
    hbm = pl.BlockSpec(memory_space=pltpu.HBM)
    edge = pltpu.HBM((tile_cols, levels, width), jnp.bfloat16)
    return pl.pallas_call(
        adjoint_kernel,
        out_shape=(
            pltpu.HBM((tiles_here, levels, width), jnp.bfloat16),
            pltpu.HBM((2 * tile_cols, levels, width), jnp.float32),
            edge,
            edge,
            pltpu.HBM((slot_count, 2, width), jnp.bfloat16),
            pltpu.HBM((tiles_here, 2, width), jnp.float32),
        ),
        in_specs=[hbm, vmem] + [hbm] * 7,
        out_specs=(hbm,) * 6,
        scratch_shapes=[
            pltpu.VMEM((tiles_here, levels, width), jnp.bfloat16),
            pltpu.VMEM((block_count, levels, width), jnp.bfloat16),
            pltpu.VMEM((block_count + 1, levels, width), jnp.float32),
            pltpu.VMEM((slot_count + 1, 2, width), jnp.bfloat16),
            pltpu.VMEM((tiles_here + 1, 2, width), jnp.float32),
            pltpu.VMEM((tiles_here, levels, width), jnp.bfloat16),
            pltpu.VMEM((2 * tile_cols, levels, width), jnp.bfloat16),
            pltpu.VMEM((KINDS, width, width), jnp.bfloat16),
            pltpu.VMEM((KINDS, width, width), jnp.bfloat16),
            pltpu.VMEM((KINDS, width, 2 * width), jnp.bfloat16),
            pltpu.VMEM((16, width), jnp.int32),
            pltpu.SMEM((tiles_here,), jnp.int32),
            pltpu.SMEM((16, width), jnp.int32),
            pltpu.SMEM((KINDS * (slot_count + UNROLL) + 1,), jnp.int32),
            pltpu.SMEM((KINDS * (slot_count + UNROLL),), jnp.int32),
            pltpu.SMEM((KINDS,), jnp.int32),
            pltpu.SemaphoreType.DMA((8,)),
            pltpu.SemaphoreType.DMA,
            pltpu.SemaphoreType.DMA((6 + PARTS,)),
        ],
        compiler_params=pltpu.CompilerParams(vmem_limit_bytes=VMEM_LIMIT),
        name="adjoint",
    )(
        in_hbm(places), received, in_hbm(adjoint), in_hbm(old), in_hbm(before), in_hbm(after),
        in_hbm(blend), in_hbm(east), in_hbm(north),
    )


def hold_kernel(edge_own, sensed_home, own, home, sem):
    copies = [
        pltpu.make_async_copy(edge_own, own, sem.at[0]),
        pltpu.make_async_copy(sensed_home, home, sem.at[1]),
    ]
    for copy in copies:
        copy.start()
    for copy in copies:
        copy.wait()


def hold(edge_own, sensed_home):
    vmem = pl.BlockSpec(memory_space=pltpu.VMEM)
    hbm = pl.BlockSpec(memory_space=pltpu.HBM)
    return pl.pallas_call(
        hold_kernel,
        out_shape=(
            pltpu.VMEM(edge_own.shape, edge_own.dtype),
            pltpu.VMEM(sensed_home.shape, sensed_home.dtype),
        ),
        in_specs=[hbm, hbm],
        out_specs=(vmem, vmem),
        scratch_shapes=[pltpu.SemaphoreType.DMA((2,))],
        compiler_params=pltpu.CompilerParams(vmem_limit_bytes=8 * 1024 * 1024),
        name="hold",
    )(in_hbm(edge_own), in_hbm(sensed_home))


def finish_kernel(
    places_all, returned, sensed_home, own, from_before, from_after, _, result, sensed, edges, out, places, sem
):
    where = pltpu.make_async_copy(places_all, places, sem.at[4])
    where.start()
    half = sensed.shape[0] // 2
    tiles_here = sensed.shape[0]
    tile_cols = from_before.shape[0]
    for c in range(tile_cols):
        edges[c] = (own[c] + from_before[c].astype(jnp.float32)).astype(jnp.bfloat16)
        edges[tile_cols + c] = (own[tile_cols + c] + from_after[c].astype(jnp.float32)).astype(jnp.bfloat16)
    copies = [
        pltpu.make_async_copy(edges.at[pl.ds(0, tile_cols)], result.at[pl.ds(0, tile_cols)], sem.at[0]),
        pltpu.make_async_copy(
            edges.at[pl.ds(tile_cols, tile_cols)],
            result.at[pl.ds(tiles_here - tile_cols, tile_cols)],
            sem.at[1],
        ),
        *[
            pltpu.make_async_copy(out.at[pl.ds(h * half, half)], sensed.at[pl.ds(h * half, half)], sem.at[2 + h])
            for h in range(2)
        ],
    ]
    copies[0].start()
    copies[1].start()
    where.wait()

    def place_some(n, carry):
        for u in range(8):
            t = n * 8 + u
            place = places[t]
            out[t] = jnp.where(place < 0, sensed_home[t], returned[jnp.maximum(place, 0)].astype(jnp.float32))
        return carry

    for h in range(2):
        lax.fori_loop(h * half // 8, (h + 1) * half // 8, place_some, 0)
        copies[2 + h].start()
    for copy in copies:
        copy.wait()


def finish(places, returned, sensed_home, own, from_before, from_after, partial):
    tiles_here, levels, width = partial.shape
    tile_cols = from_before.shape[0]
    vmem = pl.BlockSpec(memory_space=pltpu.VMEM)
    hbm = pl.BlockSpec(memory_space=pltpu.HBM)
    return pl.pallas_call(
        finish_kernel,
        out_shape=(
            pltpu.HBM(partial.shape, partial.dtype),
            pltpu.HBM((tiles_here, 2, width), jnp.float32),
        ),
        in_specs=[hbm] + [vmem] * 5 + [hbm],
        out_specs=(hbm, hbm),
        scratch_shapes=[
            pltpu.VMEM((2 * tile_cols, levels, width), jnp.bfloat16),
            pltpu.VMEM((tiles_here, 2, width), jnp.float32),
            pltpu.SMEM((tiles_here,), jnp.int32),
            pltpu.SemaphoreType.DMA((5,)),
        ],
        input_output_aliases={6: 0},
        compiler_params=pltpu.CompilerParams(vmem_limit_bytes=8 * 1024 * 1024),
        name="finish",
    )(in_hbm(places), in_vmem(returned), in_vmem(sensed_home), in_vmem(own), from_before, from_after, partial)


def on_device(
    tracer_adjoint, tracer_old, owner_lon, row_step, owner_column, tile_kind, blend_weights, slope_east, slope_north
):
    lon_count = lax.axis_size("lon")
    lat_count = lax.axis_size("lat")
    tile_rows, tile_cols = owner_lon.shape
    levels, width = tracer_adjoint.shape[2:]
    tiles_here = tile_rows * tile_cols
    north_to_south = [(i, i + 1) for i in range(lat_count - 1)]
    south_to_north = [(j, i) for i, j in north_to_south]
    adjoint = tracer_adjoint.reshape(tiles_here, levels, width)
    old = tracer_old.reshape(tiles_here, levels, width)

    send, places = pack(owner_lon.T, row_step.T, owner_column.T, tile_kind.T, adjoint, lon_count)
    received = lax.all_to_all(send, "lon", split_axis=0, concat_axis=0, tiled=True)
    before = lax.ppermute(old[-tile_cols:], "lat", north_to_south)
    after = lax.ppermute(old[:tile_cols], "lat", south_to_north)
    partial, edge_own, cross_before, cross_after, sensed_remote, sensed_home = adjoint_step(
        places, received, adjoint, old, before, after, blend_weights, slope_east, slope_north
    )
    returned = lax.all_to_all(sensed_remote, "lon", split_axis=0, concat_axis=0, tiled=True)
    from_after = lax.ppermute(cross_before, "lat", south_to_north)
    from_before = lax.ppermute(cross_after, "lat", north_to_south)
    own, home = hold(edge_own, sensed_home)
    result, sensed = finish(places, returned, home, own, from_before, from_after, partial)
    return (
        result.reshape(tracer_old.shape),
        sensed.reshape(tile_rows, tile_cols, 2, width),
    )


def solution(mesh):
    return jax.shard_map(
        on_device,
        mesh=mesh,
        in_specs=(
            P("lat", "lon", None, None),
            P("lat", "lon", None, None),
            P("lat", "lon"),
            P("lat", "lon"),
            P("lat", "lon"),
            P("lat", "lon"),
            P(),
            P(),
            P(),
        ),
        out_specs=(P("lat", "lon", None, None), P("lat", "lon", None, None)),
        check_vma=False,
    )
```

```python
import functools

import jax
import jax.numpy as jnp
from jax import lax
from jax.experimental import pallas as pl
from jax.experimental.pallas import tpu as pltpu
from jax.sharding import PartitionSpec as P

CAP = 4
META = 16
KINDS = 4
CODES = 512
EXACT = 200
UNROLL = 16
REST = 4
PARTS = 4
VMEM_LIMIT = 24 * 1024 * 1024


def in_hbm(array):
    return pltpu.with_memory_space_constraint(array, pltpu.HBM)


def in_vmem(array):
    return pltpu.with_memory_space_constraint(array, pltpu.VMEM)


def pack_kernel(
    owner_all, step_all, column_all, kind_all, adjoint, send, places,
    owner, step, column, kind, counts, rows, tiles, meta, list_sem, load_sem, sem, meta_sem,
):
    tile_cols, tile_rows = owner.shape
    tiles_here, levels, _ = adjoint.shape
    lon_count = counts.shape[0]
    me = lax.axis_index("lon")
    wholes = (owner_all, step_all, column_all, kind_all)
    lists = [
        pltpu.make_async_copy(whole, rows.at[n], list_sem.at[n]) for n, whole in enumerate(wholes)
    ]
    asks = [
        pltpu.make_async_copy(whole, here, load_sem.at[n])
        for n, (whole, here) in enumerate(zip(wholes, (owner, step, column, kind)))
    ]
    for ask in lists + asks:
        ask.start()
    load = pltpu.make_async_copy(adjoint, tiles, load_sem.at[len(asks)])
    load.start()

    for d in range(lon_count):
        counts[d] = 0
    for ask in lists:
        ask.wait()

    wide = (lon_count, tile_rows)
    device = lax.broadcasted_iota(jnp.int32, wide, 0)
    named, asked = [], []
    for j in range(tile_cols):
        to = jnp.broadcast_to(rows[0, j : j + 1, :], wide)
        block = (lax.broadcasted_iota(jnp.int32, (1, tile_rows), 1) + rows[1, j : j + 1, :]) * tile_cols
        code = (block + rows[2, j : j + 1, :]) * KINDS + rows[3, j : j + 1, :] + 1
        named.append((to == device) & (to != me))
        asked.append(jnp.broadcast_to(code, wide))
    square = (tile_rows, tile_rows)
    earlier = lax.broadcasted_iota(jnp.int32, square, 0) < lax.broadcasted_iota(jnp.int32, square, 1)
    in_row = sum(n.astype(jnp.float32) for n in named)
    rank = jnp.dot(
        in_row.astype(jnp.bfloat16), earlier.astype(jnp.bfloat16), preferred_element_type=jnp.float32
    ).astype(jnp.int32)
    lane = lax.broadcasted_iota(jnp.int32, (lon_count, meta.shape[2]), 1)
    spread = jnp.zeros(lane.shape, jnp.float32)
    ranks = []
    for j in range(tile_cols):
        ranks.append(rank)
        rank = rank + named[j].astype(jnp.int32)
    for r in range(CAP):
        of_rank = sum(
            jnp.where(named[j] & (ranks[j] == r), asked[j], 0).astype(jnp.float32) for j in range(tile_cols)
        )
        of_rank = jnp.sum(of_rank, axis=1, keepdims=True)
        spread = jnp.where(lane % CAP == r, of_rank, spread)
    mine = lane // CAP == lax.broadcasted_iota(jnp.int32, lane.shape, 0)
    line = jnp.sum(jnp.where(mine, spread, 0.0), axis=0, keepdims=True)
    line = jnp.where(line > EXACT, EXACT - line, line)
    line = jnp.broadcast_to(line, (META, meta.shape[2])).astype(jnp.bfloat16)
    for d in range(lon_count):
        meta[d] = line
    told = pltpu.make_async_copy(meta, send.at[:, pl.ds(CAP * levels, META), :], meta_sem)
    told.start()
    for ask in asks:
        ask.wait()
    load.wait()

    def send_rows(n, sent):
        for u in range(4):
            i = n * 4 + u
            for j in range(tile_cols):
                tile = i * tile_cols + j
                to = owner[j, i]
                rank = counts[to]
                remote = to != me
                counts[to] = rank + 1
                code = ((i + step[j, i]) * tile_cols + column[j, i]) * KINDS + kind[j, i] + 1
                slot = to * CAP + rank
                places[tile] = jnp.where(remote, slot, -code)

                @pl.when(remote)
                def _():
                    rows = pl.ds(pl.multiple_of(rank * levels, levels), levels)
                    pltpu.make_async_copy(tiles.at[tile], send.at[to, rows, :], sem).start()

                sent = sent + remote.astype(jnp.int32)
        return sent

    sent = lax.fori_loop(0, tile_rows // 4, send_rows, 0)
    def settle(_, carry):
        pltpu.make_async_copy(tiles.at[0], send.at[0, pl.ds(0, levels), :], sem).wait()
        return carry

    lax.fori_loop(0, sent, settle, 0)
    told.wait()


def pack(owner, step, column, kind, adjoint, lon_count):
    tiles_here, levels, width = adjoint.shape
    smem = pl.BlockSpec(memory_space=pltpu.SMEM)
    hbm = pl.BlockSpec(memory_space=pltpu.HBM)
    return pl.pallas_call(
        pack_kernel,
        out_shape=(
            pltpu.HBM((lon_count, CAP * levels + META, width), jnp.bfloat16),
            jax.ShapeDtypeStruct((tiles_here,), jnp.int32),
        ),
        in_specs=[hbm] * 5,
        out_specs=(hbm, smem),
        scratch_shapes=[
            pltpu.SMEM(owner.shape, jnp.int32),
            pltpu.SMEM(owner.shape, jnp.int32),
            pltpu.SMEM(owner.shape, jnp.int32),
            pltpu.SMEM(owner.shape, jnp.int32),
            pltpu.SMEM((lon_count,), jnp.int32),
            pltpu.VMEM((4,) + owner.shape, jnp.int32),
            pltpu.VMEM((tiles_here, levels, width), jnp.bfloat16),
            pltpu.VMEM((lon_count, META, width), jnp.bfloat16),
            pltpu.SemaphoreType.DMA((4,)),
            pltpu.SemaphoreType.DMA((5,)),
            pltpu.SemaphoreType.DMA,
            pltpu.SemaphoreType.DMA,
        ],
        compiler_params=pltpu.CompilerParams(vmem_limit_bytes=60 * 1024 * 1024),
        name="pack",
    )(in_hbm(owner), in_hbm(step), in_hbm(column), in_hbm(kind), in_hbm(adjoint))


def adjoint_kernel(
    places_all, received, adjoint, old, before, after, blend_all, east_all, north_all,
    result, edge_own, cross_before, cross_after, sensed_remote, sensed_home,
    tiles, sources, sums, remote, home, rounded, edges, blend, back, slopes, listed, places, codes, work, stay, counts, sem, code_sem, out_sem,
):
    lon_count = received.shape[0]
    tiles_here, levels, width = adjoint.shape
    slot_count = lon_count * CAP
    tile_cols = before.shape[0]
    block_count = tiles_here + 2 * tile_cols
    room = slot_count + UNROLL
    me = lax.axis_index("lon")

    told = received[:, CAP * levels : CAP * levels + META, :].astype(jnp.float32)[:, 0, :]
    device = lax.broadcasted_iota(jnp.int32, (lon_count, width), 0)
    spot = lax.broadcasted_iota(jnp.int32, (lon_count, width), 1)
    told = jnp.where(spot // CAP == me, told, 0.0).astype(jnp.bfloat16)
    first = lax.broadcasted_iota(jnp.int32, (width, width), 0)
    second = lax.broadcasted_iota(jnp.int32, (width, width), 1)
    again = ((first - second) % CAP == 0).astype(jnp.bfloat16)
    asked = jnp.dot(told, again, preferred_element_type=jnp.float32)
    code = jnp.sum(jnp.where(spot // CAP == device, asked, 0.0), axis=0, keepdims=True).astype(jnp.int32)
    code = jnp.where(code < 0, EXACT - code, code)
    row = lax.broadcasted_iota(jnp.int32, (8, width), 0)
    lane = lax.broadcasted_iota(jnp.int32, (8, width), 1)
    source_device = lane // CAP
    chosen = (code > 0) & (source_device != me) & (((code - 1) & (KINDS - 1)) == row)
    member = chosen.astype(jnp.float32)
    earlier = first < second
    before_it = jnp.dot(
        member.astype(jnp.bfloat16), earlier.astype(jnp.bfloat16), preferred_element_type=jnp.float32
    ).astype(jnp.int32)
    put_at = jnp.sum(jnp.where(chosen, row * room + before_it + 1, 0), axis=0, keepdims=True)
    put_at = jnp.where(put_at > 0, put_at - 1, KINDS * room)
    total = jnp.sum(member, axis=1, keepdims=True).astype(jnp.int32)
    listed[0:8, :] = jnp.where(row == 0, put_at, jnp.where(row == 1, lane * CODES + code - 1, 0))
    listed[8:16, :] = jnp.broadcast_to(total, (8, width))
    code_copy = pltpu.make_async_copy(listed, codes, code_sem)
    code_copy.start()
    loads = [
        pltpu.make_async_copy(old, sources.at[pl.ds(tile_cols, tiles_here)], sem.at[0]),
        pltpu.make_async_copy(before, sources.at[pl.ds(0, tile_cols)], sem.at[1]),
        pltpu.make_async_copy(after, sources.at[pl.ds(tile_cols + tiles_here, tile_cols)], sem.at[2]),
        pltpu.make_async_copy(adjoint, tiles, sem.at[3]),
    ]
    weights = [
        pltpu.make_async_copy(blend_all, blend, sem.at[4]),
        pltpu.make_async_copy(east_all, slopes.at[:, :, pl.ds(0, width)], sem.at[5]),
        pltpu.make_async_copy(north_all, slopes.at[:, :, pl.ds(width, width)], sem.at[6]),
        pltpu.make_async_copy(places_all, places, sem.at[7]),
    ]
    for copy in weights:
        copy.start()
    for copy in loads:
        copy.start()
    def clear(b, carry):
        sums[b] = jnp.zeros((levels, width), jnp.float32)
        return carry

    lax.fori_loop(0, block_count + 1, clear, 0, unroll=3)

    for copy in weights:
        copy.wait()
    for k in range(KINDS):
        back[k] = blend[k].T

    for k in range(KINDS):
        counts[k] = 0

    def enlist_home(n, carry):
        for u in range(8):
            place = places[n * 8 + u]
            code = -place - 1
            kind = code & (KINDS - 1)
            count = counts[kind]
            stay[kind * room + count] = (n * 8 + u) * CODES + code
            counts[kind] = count + (place < 0).astype(jnp.int32)
        return carry

    lax.fori_loop(0, tiles_here // 8, enlist_home, 0)
    code_copy.wait()
    for slot in range(slot_count):
        work[codes[0, slot]] = codes[1, slot]
    arrived_count = [codes[8 + k, 0] for k in range(KINDS)]
    stay_count = [counts[k] for k in range(KINDS)]
    for k in range(KINDS):
        for u in range(UNROLL):
            work[k * room + arrived_count[k] + u] = slot_count * CODES + block_count * KINDS + k
            stay[k * room + stay_count[k] + u] = tiles_here * CODES + block_count * KINDS + k
    for copy in loads[:3]:
        copy.wait()

    def arrived_tile(p):
        p = jnp.minimum(p, slot_count - 1)
        rows = pl.ds(pl.multiple_of((p & (CAP - 1)) * levels, levels), levels)
        return received[p // CAP, rows, :]

    def home_tile(p):
        return tiles[jnp.minimum(p, tiles_here - 1)]

    def some_tiles(kind, entries, tile_at, sensed):
        place = [e // CODES for e in entries]
        block = [(e & (CODES - 1)) // KINDS for e in entries]
        arrived = [tile_at(p) for p in place]
        source = [sources[jnp.minimum(b, block_count - 1)] for b in block]
        spread = jnp.dot(jnp.concatenate(arrived, axis=0), back[kind], preferred_element_type=jnp.float32)
        slope = jnp.dot(jnp.concatenate(source, axis=0), slopes[kind], preferred_element_type=jnp.float32)
        for u in range(len(entries)):
            full = arrived[u].astype(jnp.float32)
            s = slope[u * levels : (u + 1) * levels]
            both = [jnp.sum(full * part, axis=0, keepdims=True) for part in (s[:, :width], s[:, width:])]
            sensed[place[u]] = jnp.concatenate(both, axis=0).astype(sensed.dtype)
        for u in range(len(entries)):
            s = spread[u * levels : (u + 1) * levels]
            sums[block[u]] += s.astype(jnp.bfloat16).astype(jnp.float32)

    for where, (listing, many, tile_at, sensed) in enumerate((
        (work, arrived_count, arrived_tile, remote),
        (stay, stay_count, home_tile, home),
    )):
        if where == 1:
            loads[3].wait()
        for kind in range(KINDS):

            def step(n, first, kind=kind, listing=listing, tile_at=tile_at, sensed=sensed, wide=UNROLL):
                entries = [listing[kind * room + first + u] for u in range(wide)]
                some_tiles(kind, entries, tile_at, sensed)
                return first + wide

            done = lax.fori_loop(0, many[kind] // UNROLL, step, 0)
            rest = (many[kind] - done + REST - 1) // REST
            lax.fori_loop(0, rest, functools.partial(step, wide=REST), done)

    copies = []

    def put(source, target):
        copy = pltpu.make_async_copy(source, target, out_sem.at[len(copies)])
        copy.start()
        copies.append(copy)

    put(remote.at[pl.ds(0, slot_count)], sensed_remote)
    put(home.at[pl.ds(0, tiles_here)], sensed_home)
    put(sums.at[pl.ds(tile_cols, tile_cols)], edge_own.at[pl.ds(0, tile_cols)])
    put(sums.at[pl.ds(tiles_here, tile_cols)], edge_own.at[pl.ds(tile_cols, tile_cols)])

    def finish(b, carry):
        rounded[b] = sums[tile_cols + b].astype(jnp.bfloat16)
        return carry

    part = (tiles_here - 2 * tile_cols) // PARTS
    for p in range(PARTS):
        first = tile_cols + p * part
        lax.fori_loop(first, first + part, finish, 0, unroll=3)
        put(rounded.at[pl.ds(first, part)], result.at[pl.ds(first, part)])
    for c in range(tile_cols):
        edges[c] = sums[c].astype(jnp.bfloat16)
        edges[tile_cols + c] = sums[tile_cols + tiles_here + c].astype(jnp.bfloat16)
    put(edges.at[pl.ds(0, tile_cols)], cross_before)
    put(edges.at[pl.ds(tile_cols, tile_cols)], cross_after)
    for copy in copies:
        copy.wait()


def adjoint_step(places, received, adjoint, old, before, after, blend, east, north):
    lon_count = received.shape[0]
    slot_count = lon_count * CAP
    tiles_here, levels, width = adjoint.shape
    tile_cols = before.shape[0]
    block_count = tiles_here + 2 * tile_cols
    assert (block_count + 1) * KINDS <= CODES and block_count * KINDS <= EXACT + 256
    assert slot_count == width and KINDS <= 8 and tiles_here <= slot_count
    vmem = pl.BlockSpec(memory_space=pltpu.VMEM)
    hbm = pl.BlockSpec(memory_space=pltpu.HBM)
    edge = pltpu.HBM((tile_cols, levels, width), jnp.bfloat16)
    return pl.pallas_call(
        adjoint_kernel,
        out_shape=(
            pltpu.HBM((tiles_here, levels, width), jnp.bfloat16),
            pltpu.HBM((2 * tile_cols, levels, width), jnp.float32),
            edge,
            edge,
            pltpu.HBM((slot_count, 2, width), jnp.bfloat16),
            pltpu.HBM((tiles_here, 2, width), jnp.float32),
        ),
        in_specs=[hbm, vmem] + [hbm] * 7,
        out_specs=(hbm,) * 6,
        scratch_shapes=[
            pltpu.VMEM((tiles_here, levels, width), jnp.bfloat16),
            pltpu.VMEM((block_count, levels, width), jnp.bfloat16),
            pltpu.VMEM((block_count + 1, levels, width), jnp.float32),
            pltpu.VMEM((slot_count + 1, 2, width), jnp.bfloat16),
            pltpu.VMEM((tiles_here + 1, 2, width), jnp.float32),
            pltpu.VMEM((tiles_here, levels, width), jnp.bfloat16),
            pltpu.VMEM((2 * tile_cols, levels, width), jnp.bfloat16),
            pltpu.VMEM((KINDS, width, width), jnp.bfloat16),
            pltpu.VMEM((KINDS, width, width), jnp.bfloat16),
            pltpu.VMEM((KINDS, width, 2 * width), jnp.bfloat16),
            pltpu.VMEM((16, width), jnp.int32),
            pltpu.SMEM((tiles_here,), jnp.int32),
            pltpu.SMEM((16, width), jnp.int32),
            pltpu.SMEM((KINDS * (slot_count + UNROLL) + 1,), jnp.int32),
            pltpu.SMEM((KINDS * (slot_count + UNROLL),), jnp.int32),
            pltpu.SMEM((KINDS,), jnp.int32),
            pltpu.SemaphoreType.DMA((8,)),
            pltpu.SemaphoreType.DMA,
            pltpu.SemaphoreType.DMA((6 + PARTS,)),
        ],
        compiler_params=pltpu.CompilerParams(vmem_limit_bytes=VMEM_LIMIT),
        name="adjoint",
    )(
        in_hbm(places), received, in_hbm(adjoint), in_hbm(old), in_hbm(before), in_hbm(after),
        in_hbm(blend), in_hbm(east), in_hbm(north),
    )


def hold_kernel(edge_own, sensed_home, own, home, sem):
    copies = [
        pltpu.make_async_copy(edge_own, own, sem.at[0]),
        pltpu.make_async_copy(sensed_home, home, sem.at[1]),
    ]
    for copy in copies:
        copy.start()
    for copy in copies:
        copy.wait()


def hold(edge_own, sensed_home):
    vmem = pl.BlockSpec(memory_space=pltpu.VMEM)
    hbm = pl.BlockSpec(memory_space=pltpu.HBM)
    return pl.pallas_call(
        hold_kernel,
        out_shape=(
            pltpu.VMEM(edge_own.shape, edge_own.dtype),
            pltpu.VMEM(sensed_home.shape, sensed_home.dtype),
        ),
        in_specs=[hbm, hbm],
        out_specs=(vmem, vmem),
        scratch_shapes=[pltpu.SemaphoreType.DMA((2,))],
        compiler_params=pltpu.CompilerParams(vmem_limit_bytes=8 * 1024 * 1024),
        name="hold",
    )(in_hbm(edge_own), in_hbm(sensed_home))


def finish_kernel(
    places_all, returned, sensed_home, own, from_before, from_after, _, result, sensed, edges, out, places, sem
):
    where = pltpu.make_async_copy(places_all, places, sem.at[4])
    where.start()
    half = sensed.shape[0] // 2
    tiles_here = sensed.shape[0]
    tile_cols = from_before.shape[0]
    for c in range(tile_cols):
        edges[c] = (own[c] + from_before[c].astype(jnp.float32)).astype(jnp.bfloat16)
        edges[tile_cols + c] = (own[tile_cols + c] + from_after[c].astype(jnp.float32)).astype(jnp.bfloat16)
    copies = [
        pltpu.make_async_copy(edges.at[pl.ds(0, tile_cols)], result.at[pl.ds(0, tile_cols)], sem.at[0]),
        pltpu.make_async_copy(
            edges.at[pl.ds(tile_cols, tile_cols)],
            result.at[pl.ds(tiles_here - tile_cols, tile_cols)],
            sem.at[1],
        ),
        *[
            pltpu.make_async_copy(out.at[pl.ds(h * half, half)], sensed.at[pl.ds(h * half, half)], sem.at[2 + h])
            for h in range(2)
        ],
    ]
    copies[0].start()
    copies[1].start()
    where.wait()

    def place_some(n, carry):
        for u in range(8):
            t = n * 8 + u
            place = places[t]
            out[t] = jnp.where(place < 0, sensed_home[t], returned[jnp.maximum(place, 0)].astype(jnp.float32))
        return carry

    for h in range(2):
        lax.fori_loop(h * half // 8, (h + 1) * half // 8, place_some, 0)
        copies[2 + h].start()
    for copy in copies:
        copy.wait()


def finish(places, returned, sensed_home, own, from_before, from_after, partial):
    tiles_here, levels, width = partial.shape
    tile_cols = from_before.shape[0]
    vmem = pl.BlockSpec(memory_space=pltpu.VMEM)
    hbm = pl.BlockSpec(memory_space=pltpu.HBM)
    return pl.pallas_call(
        finish_kernel,
        out_shape=(
            pltpu.HBM(partial.shape, partial.dtype),
            pltpu.HBM((tiles_here, 2, width), jnp.float32),
        ),
        in_specs=[hbm] + [vmem] * 5 + [hbm],
        out_specs=(hbm, hbm),
        scratch_shapes=[
            pltpu.VMEM((2 * tile_cols, levels, width), jnp.bfloat16),
            pltpu.VMEM((tiles_here, 2, width), jnp.float32),
            pltpu.SMEM((tiles_here,), jnp.int32),
            pltpu.SemaphoreType.DMA((5,)),
        ],
        input_output_aliases={6: 0},
        compiler_params=pltpu.CompilerParams(vmem_limit_bytes=8 * 1024 * 1024),
        name="finish",
    )(in_hbm(places), in_vmem(returned), in_vmem(sensed_home), in_vmem(own), from_before, from_after, partial)


def on_device(
    tracer_adjoint, tracer_old, owner_lon, row_step, owner_column, tile_kind, blend_weights, slope_east, slope_north
):
    lon_count = lax.axis_size("lon")
    lat_count = lax.axis_size("lat")
    tile_rows, tile_cols = owner_lon.shape
    levels, width = tracer_adjoint.shape[2:]
    tiles_here = tile_rows * tile_cols
    north_to_south = [(i, i + 1) for i in range(lat_count - 1)]
    south_to_north = [(j, i) for i, j in north_to_south]
    adjoint = tracer_adjoint.reshape(tiles_here, levels, width)
    old = tracer_old.reshape(tiles_here, levels, width)

    send, places = pack(owner_lon.T, row_step.T, owner_column.T, tile_kind.T, adjoint, lon_count)
    received = lax.all_to_all(send, "lon", split_axis=0, concat_axis=0, tiled=True)
    before = lax.ppermute(old[-tile_cols:], "lat", north_to_south)
    after = lax.ppermute(old[:tile_cols], "lat", south_to_north)
    partial, edge_own, cross_before, cross_after, sensed_remote, sensed_home = adjoint_step(
        places, received, adjoint, old, before, after, blend_weights, slope_east, slope_north
    )
    returned = lax.all_to_all(sensed_remote, "lon", split_axis=0, concat_axis=0, tiled=True)
    from_after = lax.ppermute(cross_before, "lat", south_to_north)
    from_before = lax.ppermute(cross_after, "lat", north_to_south)
    own, home = hold(edge_own, sensed_home)
    result, sensed = finish(places, returned, home, own, from_before, from_after, partial)
    return (
        result.reshape(tracer_old.shape),
        sensed.reshape(tile_rows, tile_cols, 2, width),
    )


def solution(mesh):
    return jax.shard_map(
        on_device,
        mesh=mesh,
        in_specs=(
            P("lat", "lon", None, None),
            P("lat", "lon", None, None),
            P("lat", "lon"),
            P("lat", "lon"),
            P("lat", "lon"),
            P("lat", "lon"),
            P(),
            P(),
            P(),
        ),
        out_specs=(P("lat", "lon", None, None), P("lat", "lon", None, None)),
        check_vma=False,
    )
```
